128 devices in a mesh: dp: 16 (over z, y), tensor: 8 (over x, core).
Axes of the slice: x: 4, y: 4, z: 4, core: 2. Of those that a mesh axis runs over, the one named last changes fastest.
Arguments:
- grad_query: bfloat16 [16, 1, 4096, 4608], P('dp', None, 'tensor'), may hold values from -33 to 33
- grad_key: bfloat16 [16, 1, 2048, 4608], P('dp', None, 'tensor'), may hold values from -33 to 33
- error_query: bfloat16 [16, 1, 4096, 4608], P('dp', None, 'tensor'), may hold values from -12 to 12
- error_key: bfloat16 [16, 1, 2048, 4608], P('dp', None, 'tensor'), may hold values from -12 to 12
- factor_query: bfloat16 [1, 4608, 64], replicated, may hold values from -0.09375 to 0.09375
- factor_key: bfloat16 [1, 4608, 64], replicated, may hold values from -0.09375 to 0.09375
Outputs:
- error_query_new: bfloat16 [16, 1, 4096, 4608], P('dp', None, 'tensor')
- error_key_new: bfloat16 [16, 1, 2048, 4608], P('dp', None, 'tensor')
- factor_query_new: bfloat16 [1, 4608, 64], replicated
- factor_key_new: bfloat16 [1, 4608, 64], replicated
The draws below stay inside these ranges and needn't reach their ends.
All inputs are finite; a program needn't handle non-finite values.
Results may differ from the reference program's by a relative error of at most 0.0085.
Values may be sent and summed in bfloat16 or wider, within the bound.
A program may use at most 128 MiB of HBM per device.

```python
import math
import jax
import jax.numpy as jnp
from jax import lax

D = 4608
HQ = 4096
HK = 2048
RANK = 64
LAYERS = 1
REPLICAS = 16
N_DP = 16


def row_col_scales(key, salt, rows, ramp):
    key = jax.random.fold_in(key, salt)
    key_rows, key_cols = jax.random.split(key)
    row_scale = jnp.exp(jax.random.uniform(key_rows, (rows,), jnp.float32, math.log(0.3), 0.0))
    position = jnp.arange(rows, dtype=jnp.float32) / (rows - 1)
    row_scale = row_scale * jnp.power(ramp, position)
    col_scale = jnp.exp(jax.random.uniform(key_cols, (D,), jnp.float32, math.log(0.15), math.log(1.5)))
    return (row_scale, col_scale)


def shaped(key, rows, ramp, salt, amplitude):
    row_scale, col_scale = row_col_scales(key, salt, rows, ramp)
    return row_scale[:, None] * col_scale[None, :] * amplitude


def draw_grad_query(key, part):
    ramp = 3.0
    scale = shaped(key, HQ, ramp, 11, 1.0)
    key = jax.random.fold_in(key, 1)
    noise = jnp.clip(jax.random.normal(key, (REPLICAS, LAYERS, HQ, D), jnp.float32), -4.0, 4.0)
    return (noise * scale).astype(jnp.bfloat16)


def draw_grad_key(key, part):
    ramp = 3.0
    scale = shaped(key, HK, ramp, 12, 1.0)
    key = jax.random.fold_in(key, 2)
    noise = jnp.clip(jax.random.normal(key, (REPLICAS, LAYERS, HK, D), jnp.float32), -4.0, 4.0)
    return (noise * scale).astype(jnp.bfloat16)


def draw_error_query(key, part):
    ramp = 3.0
    scale = shaped(key, HQ, ramp, 11, 0.5)
    key = jax.random.fold_in(key, 3)
    noise = jnp.clip(jax.random.normal(key, (REPLICAS, LAYERS, HQ, D), jnp.float32), -4.0, 4.0)
    return (noise * scale).astype(jnp.bfloat16)


def draw_error_key(key, part):
    ramp = 3.0
    scale = shaped(key, HK, ramp, 12, 0.5)
    key = jax.random.fold_in(key, 4)
    noise = jnp.clip(jax.random.normal(key, (REPLICAS, LAYERS, HK, D), jnp.float32), -4.0, 4.0)
    return (noise * scale).astype(jnp.bfloat16)


def scatter_about(key, dims, spread, most, kind=jnp.bfloat16):
    result = spread * jax.random.normal(key, dims, jnp.float32)
    return jnp.clip(result, min=-most, max=most).astype(kind)


def setup_inputs(seed: int = 0) -> dict:
    splits = jax.random.split(jax.random.key(seed), 7)
    grad_query = draw_grad_query(jax.random.fold_in(splits[6], 71), 0)
    grad_key = draw_grad_key(jax.random.fold_in(splits[6], 71), 0)
    error_query = draw_error_query(jax.random.fold_in(splits[6], 71), 0)
    error_key = draw_error_key(jax.random.fold_in(splits[6], 71), 0)
    factor_query = scatter_about(splits[4], (LAYERS, D, RANK), D ** -0.5, 0.09375)
    factor_key = scatter_about(splits[5], (LAYERS, D, RANK), D ** -0.5, 0.09375)
    return dict(grad_query=grad_query, grad_key=grad_key, error_query=error_query, error_key=error_key, factor_query=factor_query, factor_key=factor_key)


def merge(grad, error):
    return (grad.astype(jnp.float32) + error.astype(jnp.float32)).astype(jnp.bfloat16)

def compress(grads, errors, factor):
    factor_wide = factor.astype(jnp.float32)

    def add_image(total, pair):
        merged = merge(pair[0], pair[1]).astype(jnp.float32)
        return (total + jnp.einsum('lhd,ldr->lhr', merged, factor_wide, precision=lax.Precision.HIGHEST), None)
    start = jnp.zeros((grads.shape[1], grads.shape[2], factor.shape[2]), jnp.float32)
    image, _ = lax.scan(add_image, start, (grads, errors))
    gram = jnp.einsum('lhr,lhs->lrs', image, image, precision=lax.Precision.HIGHEST)
    lower = jnp.linalg.cholesky(gram)
    solved = jax.scipy.linalg.solve_triangular(lower, jnp.swapaxes(image, 1, 2), lower=True)
    basis = jnp.swapaxes(solved, 1, 2).astype(jnp.bfloat16)
    basis_wide = basis.astype(jnp.float32)

    def add_factor(total, pair):
        merged = merge(pair[0], pair[1]).astype(jnp.float32)
        return (total + jnp.einsum('lhd,lhr->ldr', merged, basis_wide, precision=lax.Precision.HIGHEST), None)
    start_factor = jnp.zeros((grads.shape[1], grads.shape[3], factor.shape[2]), jnp.float32)
    summed, _ = lax.scan(add_factor, start_factor, (grads, errors))
    factor_new = summed.astype(jnp.bfloat16)
    approx = jnp.einsum('lhr,ldr->lhd', basis_wide, factor_new.astype(jnp.float32), precision=lax.Precision.HIGHEST)

    def refresh(pair):
        merged = merge(pair[0], pair[1]).astype(jnp.float32)
        return (merged - approx / N_DP).astype(jnp.bfloat16)
    errors_new = lax.map(refresh, (grads, errors))
    return (errors_new, factor_new)

def reference(grad_query, grad_key, error_query, error_key, factor_query, factor_key):
    error_query_new, factor_query_new = compress(grad_query, error_query, factor_query)
    error_key_new, factor_key_new = compress(grad_key, error_key, factor_key)
    return (error_query_new, error_key_new, factor_query_new, factor_key_new)
```

```python
import jax
import jax.numpy as jnp
from jax import lax
from jax.experimental import pallas as pl
from jax.experimental.pallas import tpu as pltpu
from jax.sharding import PartitionSpec as P

F32, BF16 = jnp.float32, jnp.bfloat16
D, RANK = 4608, 64
RQ, RK = 512, 256
ROWS = RQ + RK
CHUNK = 768
CHUNKS = D // CHUNK
HALF = D // 2
PART = HALF // 3
LANES = PART // 2
MESH = pl.DeviceIdType.MESH


def dot(a, b, ca=1, cb=0, precision=None):
    return lax.dot_general(a, b, (((ca,), (cb,)), ((), ())), precision=precision, preferred_element_type=F32)


def at(start, size, unit):
    return pl.ds(pl.multiple_of(start, unit), size)


def factorize(gram, inv_ref):
    lane = lax.broadcasted_iota(jnp.int32, (8, 128), 1)
    row = lax.broadcasted_iota(jnp.int32, (8, 128), 0)
    side = jnp.where(lane >= RANK, RANK, 0)
    g = [gram[8 * i:8 * i + 8, :] for i in range(8)]
    w = [jnp.where(lane - side == row + 8 * i, 1.0, 0.0).astype(F32) for i in range(8)]

    def column(x, j):
        return jnp.take_along_axis(x, side + j, axis=1, mode="promise_in_bounds")

    for j in range(RANK):
        b, t = divmod(j, 8)
        row_g = jnp.broadcast_to(g[b][t:t + 1, :], (8, 128))
        row_w = jnp.broadcast_to(w[b][t:t + 1, :], (8, 128))
        pivot = column(row_g, j)
        inverse = 1.0 / pivot
        inv_ref[j:j + 1, :] = (row_w * lax.rsqrt(pivot))[0:1, :]
        scaled_g, scaled_w = row_g * inverse, row_w * inverse
        for i in range(b, 8):
            c = column(g[i], j)
            if i == b:
                c = jnp.where(row > t, c, 0.0)
            g[i] = g[i] - c * scaled_g
            w[i] = w[i] - c * scaled_w


def reduce_kernel(gq, gk, eq, ek, fq, fk, merged, basis, psum, inv,
                  ebuf, fbuf, acc, ar1, ar2, packed, image_t, image_h,
                  gsend, gsib, gx, psend, psib, pown, rs, ar3,
                  lsem, fsem, s_ar1, r_ar1, s_ar2, r_ar2, s_g, r_g, s_gx, r_gx,
                  s_p, r_p, s_rs, r_rs, s_a3, r_a3, s_ag, r_ag, s_fw, r_fw):
    dp, tensor = lax.axis_index("dp"), lax.axis_index("tensor")
    z, y = lax.div(dp, 4), lax.rem(dp, 4)
    x, c = lax.div(tensor, 2), lax.rem(tensor, 2)

    def device(dz=0, dy=0, dx=0, dc=0):
        return (lax.rem(z + dz, 4) * 4 + lax.rem(y + dy, 4), lax.rem(x + dx, 4) * 2 + lax.rem(c + dc, 2))

    def send(src, dst, ssem, rsem, to):
        pltpu.make_async_remote_copy(src, dst, ssem, rsem, device_id=to, device_id_type=MESH).start()

    def arrived(ref, rsem, ssem):
        pltpu.make_async_remote_copy(ref, ref, ssem, rsem, device_id=device(dc=1), device_id_type=MESH).wait_recv()

    def sent(ref, rsem, ssem):
        pltpu.make_async_remote_copy(ref, ref, ssem, rsem, device_id=device(dc=1), device_id_type=MESH).wait_send()

    loads = [
        pltpu.make_async_copy(fq.at[0], fbuf.at[0], fsem),
        pltpu.make_async_copy(fk.at[0], fbuf.at[1], fsem),
    ]
    for cp in loads:
        cp.start()

    def load(k):
        cols = at(k * CHUNK, CHUNK, 128)
        return [
            pltpu.make_async_copy(gq.at[0, 0, :, cols], merged.at[0:RQ, cols], lsem.at[k]),
            pltpu.make_async_copy(eq.at[0, 0, :, cols], ebuf.at[0:RQ, cols], lsem.at[k]),
            pltpu.make_async_copy(gk.at[0, 0, :, cols], merged.at[RQ:ROWS, cols], lsem.at[k]),
            pltpu.make_async_copy(ek.at[0, 0, :, cols], ebuf.at[RQ:ROWS, cols], lsem.at[k]),
        ]

    for k in range(CHUNKS):
        for cp in load(k):
            cp.start()

    offsets = [(a, b, d) for a in range(4) for b in range(4) for d in range(4) if (a, b, d) != (0, 0, 0) and 0 in (a, b, d)]
    barrier = pltpu.get_barrier_semaphore()
    peers = [device(a, b, d) for a, b, d in offsets] + [device(dc=1)]
    for to in peers:
        pl.semaphore_signal(barrier, 1, device_id=to, device_id_type=MESH)

    acc[...] = jnp.zeros_like(acc)
    for cp in loads:
        cp.wait()

    def merge(k, carry):
        cols = at(k * CHUNK, CHUNK, 128)
        for cp in load(k):
            cp.wait()
        for block in range(3):
            rows = slice(256 * block, 256 * block + 256)
            m = (merged[rows, cols].astype(F32) + ebuf[rows, cols].astype(F32)).astype(BF16)
            merged[rows, cols] = m
            acc[rows, :] += dot(m, fbuf[block // 2, :, cols], 1, 1)
        return carry

    lax.fori_loop(0, CHUNKS, merge, 0)

    halves = (ar1.at[0, z], ar1.at[1, y])
    top = jnp.concatenate([acc[0:256, :], acc[256:512, :]], axis=1).astype(BF16)
    low = jnp.concatenate([acc[512:640, :], acc[640:768, :]], axis=1).astype(BF16)
    halves[0][...] = top[0:192]
    halves[1][0:64, :] = top[192:256]
    halves[1][64:192, :] = low
    pl.semaphore_wait(barrier, len(peers))
    for d in (1, 2, 3):
        send(ar1.at[0, z], ar1.at[0, z], s_ar1.at[0], r_ar1.at[0], device(dz=d))
        send(ar1.at[1, y], ar1.at[1, y], s_ar1.at[1], r_ar1.at[1], device(dy=d))
    for h, mine in ((0, y), (1, z)):
        arrived(ar1.at[h, 0:3], r_ar1.at[h], s_ar1.at[h])
        total = ar1[h, 0].astype(F32)
        for s in (1, 2, 3):
            total += ar1[h, s].astype(F32)
        ar2[h, mine] = total.astype(BF16)
        for d in (1, 2, 3):
            to = device(dy=d) if h == 0 else device(dz=d)
            send(ar2.at[h, mine], ar2.at[h, mine], s_ar2.at[h], r_ar2.at[h], to)
    for h in (0, 1):
        arrived(ar2.at[h, 0:3], r_ar2.at[h], s_ar2.at[h])
        total = ar2[h, 0].astype(F32)
        for s in (1, 2, 3):
            total += ar2[h, s].astype(F32)
        packed[192 * h:192 * h + 192, :] = total

    flipped = packed[...].T
    tq = jnp.concatenate([flipped[0:64, 0:256], flipped[64:128, 0:256]], axis=1)
    tk = jnp.concatenate([flipped[0:64, 256:384], flipped[64:128, 256:384]], axis=1)
    image_t[:, 0:RQ] = tq
    image_t[:, RQ:ROWS] = tk
    image_h[0:64, :] = image_t[...].astype(BF16)
    image_h[64:128, :] = (image_t[...] - image_h[0:64, :].astype(F32)).astype(BF16)

    high = lax.Precision.HIGHEST
    gsend[...] = jnp.concatenate([dot(tq, tq, 1, 1, high), dot(tk, tk, 1, 1, high)], axis=1)
    send(gsend, gsib, s_g, r_g, device(dc=1))

    def project(start):
        cols = at(start, PART, 128)
        q = dot(image_h[:, 0:RQ], merged[0:RQ, cols])
        k = dot(image_h[:, RQ:ROWS], merged[RQ:ROWS, cols])
        return q[0:64] + q[64:128], k[0:64] + k[64:128]

    for k in range(3):
        q, kk = project((1 - c) * HALF + PART * k)
        psend[k, 0:64, :] = q.astype(BF16)
        psend[k, 64:128, :] = kk.astype(BF16)
        send(psend.at[k], psib.at[k], s_p.at[k], r_p.at[k], device(dc=1))

    arrived(gsib, r_g, s_g)
    gx[x] = gsend[...] + gsib[...]
    for d in (1, 2, 3):
        send(gx.at[x], gx.at[x], s_gx, r_gx, device(dx=d))

    place = ((z, y, x), (z, x, y), (y, x, z))

    def move(k, da, db):
        return (device(da, db, 0), device(da, 0, db), device(0, da, db))[k]

    def slice_of(a, b):
        return at(16 * (2 * a + lax.div(b, 2)), 16, 16), LANES * lax.rem(b, 2)

    around = [(da, db) for da in range(4) for db in range(4) if (da, db) != (0, 0)]
    for k in range(3):
        q, kk = project(c * HALF + PART * k)
        arrived(psib.at[k], r_p.at[k], s_p.at[k])
        pown[k, 0:64, :] = (q + psib[k, 0:64, :].astype(F32)).astype(BF16)
        pown[k, 64:128, :] = (kk + psib[k, 64:128, :].astype(F32)).astype(BF16)
        a, b, _ = place[k]
        for da, db in around:
            rows, lanes = slice_of(lax.rem(a + da, 4), lax.rem(b + db, 4))
            send(pown.at[k, rows, at(lanes, LANES, 128)], rs.at[k, 4 * a + b], s_rs.at[k], r_rs.at[k], move(k, da, db))
        rows, lanes = slice_of(a, b)
        rs[k, 4 * a + b] = pown[k, rows, at(lanes, LANES, 128)]

    arrived(gx.at[0:3], r_gx, s_gx)
    factorize((gx[0] + gx[1]) + (gx[2] + gx[3]), inv)

    for k in range(3):
        arrived(rs.at[k, 0:15], r_rs.at[k], s_rs.at[k])
        total = rs[k, 0].astype(F32)
        for s in range(1, 16):
            total += rs[k, s].astype(F32)
        m = place[k][2]
        ar3[k, m] = total.astype(BF16)
        for d in (1, 2, 3):
            to = (device(dx=d), device(dy=d), device(dz=d))[k]
            send(ar3.at[k, m], ar3.at[k, m], s_a3.at[k], r_a3.at[k], to)

    both = inv[...]
    bq = dot(image_t[:, 0:RQ], both[:, 0:64], 0, 1, high)
    bk = dot(image_t[:, RQ:ROWS], both[:, 64:128], 0, 1, high)
    basis[0:RQ, :] = bq.astype(BF16)
    basis[RQ:ROWS, :] = bk.astype(BF16)

    for k in range(3):
        arrived(ar3.at[k, 0:3], r_a3.at[k], s_a3.at[k])
        total = ar3[k, 0].astype(F32)
        for s in (1, 2, 3):
            total += ar3[k, s].astype(F32)
        a, b, _ = place[k]
        rows, lanes = slice_of(a, b)
        spot = (rows, at(c * HALF + PART * k + lanes, LANES, 128))
        psum[spot] = total.astype(BF16)
        for da, db in around:
            send(psum.at[spot], psum.at[spot], s_ag.at[k], r_ag.at[k], move(k, da, db))

    for k in range(3):
        arrived(rs.at[k, 0:15], r_ag.at[k], s_ag.at[k])
        cols = at(c * HALF + PART * k, PART, 128)
        send(psum.at[:, cols], psum.at[:, cols], s_fw.at[k], r_fw.at[k], device(dc=1))

    sent(gsend, r_g, s_g)
    sent(gx.at[0:3], r_gx, s_gx)
    for h in (0, 1):
        sent(ar1.at[h, 0:3], r_ar1.at[h], s_ar1.at[h])
        sent(ar2.at[h, 0:3], r_ar2.at[h], s_ar2.at[h])
    for k in range(3):
        sent(psend.at[k], r_p.at[k], s_p.at[k])
        sent(rs.at[k, 0:15], r_rs.at[k], s_rs.at[k])
        sent(ar3.at[k, 0:3], r_a3.at[k], s_a3.at[k])
        sent(rs.at[k, 0:15], r_ag.at[k], s_ag.at[k])
    for k in range(3):
        arrived(psend.at[k], r_fw.at[k], s_fw.at[k])
        sent(psend.at[k], r_fw.at[k], s_fw.at[k])


def reduce(gq, gk, eq, ek, fq, fk):
    dma, vmem = pltpu.SemaphoreType.DMA, pltpu.VMEM
    return pl.pallas_call(
        reduce_kernel,
        name="reduce",
        out_shape=(
            vmem((ROWS, D), BF16),
            vmem((ROWS, RANK), BF16),
            vmem((2 * RANK, D), BF16),
            vmem((RANK, 128), F32),
        ),
        in_specs=[pl.BlockSpec(memory_space=pltpu.HBM)] * 6,
        out_specs=(pl.BlockSpec(memory_space=vmem),) * 4,
        scratch_shapes=[
            vmem((ROWS, D), BF16),
            vmem((2, RANK, D), BF16),
            vmem((ROWS, RANK), F32),
            vmem((2, 4, 192, 128), BF16),
            vmem((2, 4, 192, 128), BF16),
            vmem((384, 128), F32),
            vmem((RANK, ROWS), F32),
            vmem((2 * RANK, ROWS), BF16),
            vmem((RANK, 128), F32),
            vmem((RANK, 128), F32),
            vmem((4, RANK, 128), F32),
            vmem((3, 128, PART), BF16),
            vmem((3, 128, PART), BF16),
            vmem((3, 128, PART), BF16),
            vmem((3, 16, 16, LANES), BF16),
            vmem((3, 4, 16, LANES), BF16),
            dma((CHUNKS,)), dma,
            dma((2,)), dma((2,)), dma((2,)), dma((2,)),
            dma, dma, dma, dma,
            dma((3,)), dma((3,)), dma((3,)), dma((3,)), dma((3,)), dma((3,)),
            dma((3,)), dma((3,)), dma((3,)), dma((3,)),
        ],
        compiler_params=pltpu.CompilerParams(
            collective_id=0, has_side_effects=True, vmem_limit_bytes=53 << 20
        ),
    )(gq, gk, eq, ek, fq, fk)


def refresh_kernel(merged, basis, psum, inv, error_q, error_k, new_q, new_k):
    both = inv[...]
    cols = at(pl.program_id(0) * CHUNK, CHUNK, 128)
    for side, rows, new, error in ((0, slice(0, RQ), new_q, error_q), (1, slice(RQ, ROWS), new_k, error_k)):
        w = both[:, 64 * side:64 * side + 64]
        hi = w.astype(BF16)
        lo = (w - hi.astype(F32)).astype(BF16)
        p = psum[64 * side:64 * side + 64, cols]
        factor = (dot(hi, p) + dot(lo, p)).astype(BF16)
        new[0] = factor
        approx = dot(basis[rows, :] * 0.0625, factor)
        error[0, 0] = (merged[rows, cols].astype(F32) - approx).astype(BF16)


def refresh(merged, basis, psum, inv):
    return pl.pallas_call(
        refresh_kernel,
        name="refresh",
        grid=(CHUNKS,),
        out_shape=(
            jax.ShapeDtypeStruct((1, 1, RQ, D), BF16),
            jax.ShapeDtypeStruct((1, 1, RK, D), BF16),
            jax.ShapeDtypeStruct((1, RANK, D), BF16),
            jax.ShapeDtypeStruct((1, RANK, D), BF16),
        ),
        in_specs=[pl.BlockSpec(memory_space=pltpu.VMEM)] * 4,
        out_specs=(
            pl.BlockSpec((1, 1, RQ, CHUNK), lambda i: (0, 0, 0, i)),
            pl.BlockSpec((1, 1, RK, CHUNK), lambda i: (0, 0, 0, i)),
            pl.BlockSpec((1, RANK, CHUNK), lambda i: (0, 0, i)),
            pl.BlockSpec((1, RANK, CHUNK), lambda i: (0, 0, i)),
        ),
        compiler_params=pltpu.CompilerParams(vmem_limit_bytes=24 << 20),
    )(merged, basis, psum, inv)


def body(grad_query, grad_key, error_query, error_key, factor_query, factor_key):
    fq, fk = jnp.swapaxes(factor_query, 1, 2), jnp.swapaxes(factor_key, 1, 2)
    kept = reduce(grad_query, grad_key, error_query, error_key, fq, fk)
    new_eq, new_ek, new_q, new_k = refresh(*kept)
    return new_eq, new_ek, jnp.swapaxes(new_q, 1, 2), jnp.swapaxes(new_k, 1, 2)


def solution(mesh):
    split = P("dp", None, "tensor", None)
    return jax.shard_map(
        body,
        mesh=mesh,
        in_specs=(split, split, split, split, P(), P()),
        out_specs=(split, split, P(), P()),
        check_vma=False,
    )
```

```python
import jax
import jax.numpy as jnp
from jax import lax
from jax.experimental import pallas as pl
from jax.experimental.pallas import tpu as pltpu
from jax.sharding import PartitionSpec as P

F32, BF16 = jnp.float32, jnp.bfloat16
D, RANK = 4608, 64
RQ, RK = 512, 256
ROWS = RQ + RK
LOADS, WIDE = 3, D // 3
HALF = D // 2
PART = HALF // 3
LANES = PART // 2
MESH = pl.DeviceIdType.MESH


def dot(a, b, ca=1, cb=0, precision=None):
    return lax.dot_general(a, b, (((ca,), (cb,)), ((), ())), precision=precision, preferred_element_type=F32)


def at(start, size, unit):
    return pl.ds(pl.multiple_of(start, unit), size)


def factorize(gram, inv):
    lane = lax.broadcasted_iota(jnp.int32, (8, 128), 1)
    row = lax.broadcasted_iota(jnp.int32, (8, 128), 0)
    side = jnp.where(lane >= RANK, RANK, 0)
    for i in range(8):
        inv[8 * i:8 * i + 8, :] = jnp.where(lane - side == row + 8 * i, 1.0, 0.0).astype(F32)

    def column(x, j):
        return jnp.take_along_axis(x, side + j, axis=1, mode="promise_in_bounds")

    def block(b, carry):
        here = at(8 * b, 8, 8)
        g = [gram[here, :]] + [gram[8 * i:8 * i + 8, :] for i in range(8)]
        w = [inv[here, :]] + [inv[8 * i:8 * i + 8, :] for i in range(8)]
        done = [None] * 8
        for t in range(8):
            row_g = jnp.broadcast_to(g[0][t:t + 1, :], (8, 128))
            row_w = jnp.broadcast_to(w[0][t:t + 1, :], (8, 128))
            pivot = column(row_g, 8 * b + t)
            inverse = 1.0 / pivot
            done[t] = row_w * lax.rsqrt(pivot)
            scaled_g, scaled_w = row_g * inverse, row_w * inverse
            for i in range(9):
                below = row > t if i == 0 else i - 1 > b
                q = jnp.where(below, column(g[i], 8 * b + t), 0.0)
                g[i] = g[i] - q * scaled_g
                w[i] = w[i] - q * scaled_w
        last = done[0]
        for t in range(1, 8):
            last = jnp.where(row == t, done[t], last)
        for i in range(8):
            gram[8 * i:8 * i + 8, :] = g[i + 1]
            inv[8 * i:8 * i + 8, :] = w[i + 1]
        inv[here, :] = last
        return carry

    lax.fori_loop(0, 8, block, 0)


def subtract(source, target, basis, factor, start, into):
    cols, there = at(start, PART, 128), at(into, PART, 128)
    for side, rows in ((0, slice(0, RQ)), (1, slice(RQ, ROWS))):
        approx = dot(basis[rows, :], factor[64 * side:64 * side + 64, cols])
        target[rows, there] = (source[rows, cols].astype(F32) - approx).astype(BF16)


def reduce_kernel(gq, gk, eq, ek, fq, fk, merged, basis, factor,
                  psum, inv, white, ebuf, fbuf, acc, ar1, ar2, packed, image_t, image_h,
                  gsend, gsib, gx, psend, psib, pown, rs, ar3,
                  lsem, fsem, s_ar1, r_ar1, s_ar2, r_ar2, s_g, r_g, s_gx, r_gx,
                  s_p, r_p, s_rs, r_rs, s_a3, r_a3, s_ag, r_ag, s_fw, r_fw):
    dp, tensor = lax.axis_index("dp"), lax.axis_index("tensor")
    z, y = lax.div(dp, 4), lax.rem(dp, 4)
    x, c = lax.div(tensor, 2), lax.rem(tensor, 2)

    def device(dz=0, dy=0, dx=0, dc=0):
        return (lax.rem(z + dz, 4) * 4 + lax.rem(y + dy, 4), lax.rem(x + dx, 4) * 2 + lax.rem(c + dc, 2))

    def send(src, dst, ssem, rsem, to):
        pltpu.make_async_remote_copy(src, dst, ssem, rsem, device_id=to, device_id_type=MESH).start()

    def arrived(ref, rsem, ssem):
        pltpu.make_async_remote_copy(ref, ref, ssem, rsem, device_id=device(dc=1), device_id_type=MESH).wait_recv()

    def sent(ref, rsem, ssem):
        pltpu.make_async_remote_copy(ref, ref, ssem, rsem, device_id=device(dc=1), device_id_type=MESH).wait_send()

    loads = [
        pltpu.make_async_copy(fq.at[0], fbuf.at[0], fsem),
        pltpu.make_async_copy(fk.at[0], fbuf.at[1], fsem),
    ]
    for cp in loads:
        cp.start()

    def load(k):
        cols = at(k * WIDE, WIDE, 128)
        return [
            pltpu.make_async_copy(gq.at[0, 0, :, cols], merged.at[0:RQ, cols], lsem.at[k]),
            pltpu.make_async_copy(eq.at[0, 0, :, cols], ebuf.at[0:RQ, cols], lsem.at[k]),
            pltpu.make_async_copy(gk.at[0, 0, :, cols], merged.at[RQ:ROWS, cols], lsem.at[k]),
            pltpu.make_async_copy(ek.at[0, 0, :, cols], ebuf.at[RQ:ROWS, cols], lsem.at[k]),
        ]

    for k in range(LOADS):
        for cp in load(k):
            cp.start()

    offsets = [(a, b, d) for a in range(4) for b in range(4) for d in range(4) if (a, b, d) != (0, 0, 0) and 0 in (a, b, d)]
    barrier = pltpu.get_barrier_semaphore()
    peers = [device(a, b, d) for a, b, d in offsets] + [device(dc=1)]
    for to in peers:
        pl.semaphore_signal(barrier, 1, device_id=to, device_id_type=MESH)

    acc[...] = jnp.zeros_like(acc)
    for cp in loads:
        cp.wait()

    def merge(k, carry):
        cols = at(k * WIDE, WIDE, 128)
        for cp in load(k):
            cp.wait()
        merged[:, cols] = (merged[:, cols].astype(F32) + ebuf[:, cols].astype(F32)).astype(BF16)
        acc[0:RQ, :] += dot(merged[0:RQ, cols], fbuf[0, :, cols], 1, 1)
        acc[RQ:ROWS, :] += dot(merged[RQ:ROWS, cols], fbuf[1, :, cols], 1, 1)
        return carry

    lax.fori_loop(0, LOADS, merge, 0)

    halves = (ar1.at[0, z], ar1.at[1, y])
    top = jnp.concatenate([acc[0:256, :], acc[256:512, :]], axis=1).astype(BF16)
    low = jnp.concatenate([acc[512:640, :], acc[640:768, :]], axis=1).astype(BF16)
    halves[0][...] = top[0:192]
    halves[1][0:64, :] = top[192:256]
    halves[1][64:192, :] = low
    pl.semaphore_wait(barrier, len(peers))
    for d in (1, 2, 3):
        send(ar1.at[0, z], ar1.at[0, z], s_ar1.at[0], r_ar1.at[0], device(dz=d))
        send(ar1.at[1, y], ar1.at[1, y], s_ar1.at[1], r_ar1.at[1], device(dy=d))
    for h, mine in ((0, y), (1, z)):
        arrived(ar1.at[h, 0:3], r_ar1.at[h], s_ar1.at[h])
        total = ar1[h, 0].astype(F32)
        for s in (1, 2, 3):
            total += ar1[h, s].astype(F32)
        ar2[h, mine] = total.astype(BF16)
        for d in (1, 2, 3):
            to = device(dy=d) if h == 0 else device(dz=d)
            send(ar2.at[h, mine], ar2.at[h, mine], s_ar2.at[h], r_ar2.at[h], to)
    for h in (0, 1):
        arrived(ar2.at[h, 0:3], r_ar2.at[h], s_ar2.at[h])
        total = ar2[h, 0].astype(F32)
        for s in (1, 2, 3):
            total += ar2[h, s].astype(F32)
        packed[192 * h:192 * h + 192, :] = total

    flipped = packed[...].T
    tq = jnp.concatenate([flipped[0:64, 0:256], flipped[64:128, 0:256]], axis=1)
    tk = jnp.concatenate([flipped[0:64, 256:384], flipped[64:128, 256:384]], axis=1)
    image_t[:, 0:RQ] = tq
    image_t[:, RQ:ROWS] = tk
    image_h[0:64, :] = image_t[...].astype(BF16)
    image_h[64:128, :] = (image_t[...] - image_h[0:64, :].astype(F32)).astype(BF16)

    def project(start):
        cols = at(start, PART, 128)
        q = dot(image_h[:, 0:RQ], merged[0:RQ, cols])
        k = dot(image_h[:, RQ:ROWS], merged[RQ:ROWS, cols])
        return q[0:64] + q[64:128], k[0:64] + k[64:128]

    def split(k):
        first, last = lax.div(2 - k, 2), lax.div(k, 2)
        return first, 1 - first - last, last

    def place(k):
        first, middle, last = split(k)
        return z * (1 - last) + y * last, y * first + x * (1 - first), x * first + y * middle + z * last

    def move(k, da, db):
        first, middle, last = split(k)
        return device(da * (1 - last), db * first + da * last, db * (1 - first))

    def along(k, d):
        first, middle, last = split(k)
        return device(d * last, d * middle, d * first)

    def slice_of(a, b):
        return at(16 * (2 * a + lax.div(b, 2)), 16, 16), LANES * lax.rem(b, 2)

    around = [(da, db) for da in range(4) for db in range(4) if (da, db) != (0, 0)]

    def share(n, carry):
        @pl.when(n < 3)
        def _():
            q, kk = project((1 - c) * HALF + PART * n)
            psend[n, 0:64, :] = q.astype(BF16)
            psend[n, 64:128, :] = kk.astype(BF16)
            send(psend.at[n], psib.at[n], s_p.at[n], r_p.at[n], device(dc=1))

        @pl.when(n > 0)
        def _():
            k = n - 1
            q, kk = project(c * HALF + PART * k)
            arrived(psib.at[k], r_p.at[k], s_p.at[k])
            pown[k, 0:64, :] = (q + psib[k, 0:64, :].astype(F32)).astype(BF16)
            pown[k, 64:128, :] = (kk + psib[k, 64:128, :].astype(F32)).astype(BF16)
            a, b, _ = place(k)
            for da, db in around:
                rows, lanes = slice_of(lax.rem(a + da, 4), lax.rem(b + db, 4))
                send(pown.at[k, rows, at(lanes, LANES, 128)], rs.at[k, 4 * a + b], s_rs.at[k], r_rs.at[k], move(k, da, db))
            rows, lanes = slice_of(a, b)
            rs[k, 4 * a + b] = pown[k, rows, at(lanes, LANES, 128)]

        return carry

    lax.fori_loop(0, 4, share, 0)

    high = lax.Precision.HIGHEST
    tq, tk = image_t[:, 0:RQ], image_t[:, RQ:ROWS]
    gsend[...] = jnp.concatenate([dot(tq, tq, 1, 1, high), dot(tk, tk, 1, 1, high)], axis=1)
    send(gsend, gsib, s_g, r_g, device(dc=1))
    arrived(gsib, r_g, s_g)
    gx[x] = gsend[...] + gsib[...]
    for d in (1, 2, 3):
        send(gx.at[x], gx.at[x], s_gx, r_gx, device(dx=d))

    def gather(k, carry):
        arrived(rs.at[k, 0:15], r_rs.at[k], s_rs.at[k])
        total = rs[k, 0].astype(F32)
        for s in range(1, 16):
            total += rs[k, s].astype(F32)
        m = place(k)[2]
        ar3[k, m] = total.astype(BF16)
        for d in (1, 2, 3):
            send(ar3.at[k, m], ar3.at[k, m], s_a3.at[k], r_a3.at[k], along(k, d))
        return carry

    lax.fori_loop(0, 3, gather, 0)

    def spread(k, carry):
        arrived(ar3.at[k, 0:3], r_a3.at[k], s_a3.at[k])
        total = ar3[k, 0].astype(F32)
        for s in (1, 2, 3):
            total += ar3[k, s].astype(F32)
        a, b, _ = place(k)
        rows, lanes = slice_of(a, b)
        spot = (rows, at(c * HALF + PART * k + lanes, LANES, 128))
        psum[spot] = total.astype(BF16)
        for da, db in around:
            send(psum.at[spot], psum.at[spot], s_ag.at[k], r_ag.at[k], move(k, da, db))
        return carry

    lax.fori_loop(0, 3, spread, 0)

    arrived(gx.at[0:3], r_gx, s_gx)
    gsib[...] = (gx[0] + gx[1]) + (gx[2] + gx[3])
    factorize(gsib, inv)
    both = inv[...]
    for side, rows in ((0, slice(0, RQ)), (1, slice(RQ, ROWS))):
        w = both[:, 64 * side:64 * side + 64]
        basis[rows, :] = dot(image_t[:, rows], w, 0, 1, high).astype(BF16) * 0.0625
        hi = w.astype(BF16)
        white[side, 0:64] = hi
        white[side, 64:128] = (w - hi.astype(F32)).astype(BF16)

    def whiten(k, carry):
        arrived(rs.at[k, 0:15], r_ag.at[k], s_ag.at[k])
        cols = at(c * HALF + PART * k, PART, 128)
        for side in (0, 1):
            f = dot(white[side], psum[64 * side:64 * side + 64, cols])
            factor[64 * side:64 * side + 64, cols] = (f[0:64] + f[64:128]).astype(BF16)
        send(factor.at[:, cols], factor.at[:, cols], s_fw.at[k], r_fw.at[k], device(dc=1))
        return carry

    lax.fori_loop(0, 3, whiten, 0)

    def errors(k, carry):
        start = c * HALF + PART * k
        subtract(merged, merged, basis, factor, start, start)
        return carry

    lax.fori_loop(0, 3, errors, 0)

    sent(gsend, r_g, s_g)
    sent(gx.at[0:3], r_gx, s_gx)
    for h in (0, 1):
        sent(ar1.at[h, 0:3], r_ar1.at[h], s_ar1.at[h])
        sent(ar2.at[h, 0:3], r_ar2.at[h], s_ar2.at[h])
    for k in range(3):
        sent(psend.at[k], r_p.at[k], s_p.at[k])
        sent(rs.at[k, 0:15], r_rs.at[k], s_rs.at[k])
        sent(ar3.at[k, 0:3], r_a3.at[k], s_a3.at[k])
        sent(rs.at[k, 0:15], r_ag.at[k], s_ag.at[k])
    for k in range(3):
        arrived(psend.at[k], r_fw.at[k], s_fw.at[k])
        sent(psend.at[k], r_fw.at[k], s_fw.at[k])


def reduce(gq, gk, eq, ek, fq, fk):
    dma, vmem = pltpu.SemaphoreType.DMA, pltpu.VMEM
    return pl.pallas_call(
        reduce_kernel,
        name="reduce",
        out_shape=(
            vmem((ROWS, D), BF16),
            vmem((ROWS, RANK), BF16),
            vmem((2 * RANK, D), BF16),
        ),
        in_specs=[pl.BlockSpec(memory_space=pltpu.HBM)] * 6,
        out_specs=(pl.BlockSpec(memory_space=vmem),) * 3,
        scratch_shapes=[
            vmem((2 * RANK, D), BF16),
            vmem((RANK, 128), F32),
            vmem((2, 128, RANK), BF16),
            vmem((ROWS, D), BF16),
            vmem((2, RANK, D), BF16),
            vmem((ROWS, RANK), F32),
            vmem((2, 4, 192, 128), BF16),
            vmem((2, 4, 192, 128), BF16),
            vmem((384, 128), F32),
            vmem((RANK, ROWS), F32),
            vmem((2 * RANK, ROWS), BF16),
            vmem((RANK, 128), F32),
            vmem((RANK, 128), F32),
            vmem((4, RANK, 128), F32),
            vmem((3, 128, PART), BF16),
            vmem((3, 128, PART), BF16),
            vmem((3, 128, PART), BF16),
            vmem((3, 16, 16, LANES), BF16),
            vmem((3, 4, 16, LANES), BF16),
            dma((LOADS,)), dma,
            dma((2,)), dma((2,)), dma((2,)), dma((2,)),
            dma, dma, dma, dma,
            dma((3,)), dma((3,)), dma((3,)), dma((3,)), dma((3,)), dma((3,)),
            dma((3,)), dma((3,)), dma((3,)), dma((3,)),
        ],
        compiler_params=pltpu.CompilerParams(
            collective_id=0, has_side_effects=True, vmem_limit_bytes=53 << 20
        ),
    )(gq, gk, eq, ek, fq, fk)


def refresh_kernel(merged, basis, factor, error_q, error_k, new_q, new_k, buf, sem):
    c = lax.rem(lax.axis_index("tensor"), 2)
    own, other = c * HALF, (1 - c) * HALF
    mine = at(own, HALF, 128)
    copies = [
        pltpu.make_async_copy(merged.at[0:RQ, mine], error_q.at[0, 0, :, mine], sem.at[0]),
        pltpu.make_async_copy(merged.at[RQ:ROWS, mine], error_k.at[0, 0, :, mine], sem.at[1]),
        pltpu.make_async_copy(factor.at[0:RANK], new_q.at[0], sem.at[2]),
        pltpu.make_async_copy(factor.at[RANK:2 * RANK], new_k.at[0], sem.at[3]),
    ]
    for cp in copies:
        cp.start()
    def part(k):
        here, there = at(PART * k, PART, 128), at(other + PART * k, PART, 128)
        return [
            pltpu.make_async_copy(buf.at[0:RQ, here], error_q.at[0, 0, :, there], sem.at[4 + 2 * k]),
            pltpu.make_async_copy(buf.at[RQ:ROWS, here], error_k.at[0, 0, :, there], sem.at[5 + 2 * k]),
        ]

    def errors(k, carry):
        subtract(merged, buf, basis, factor, other + PART * k, PART * k)
        for cp in part(k):
            cp.start()
        return carry

    lax.fori_loop(0, 3, errors, 0)
    for k in range(3):
        copies += part(k)
    for cp in copies:
        cp.wait()


def refresh(merged, basis, factor):
    return pl.pallas_call(
        refresh_kernel,
        name="refresh",
        out_shape=(
            jax.ShapeDtypeStruct((1, 1, RQ, D), BF16),
            jax.ShapeDtypeStruct((1, 1, RK, D), BF16),
            jax.ShapeDtypeStruct((1, RANK, D), BF16),
            jax.ShapeDtypeStruct((1, RANK, D), BF16),
        ),
        in_specs=[pl.BlockSpec(memory_space=pltpu.VMEM)] * 3,
        out_specs=(pl.BlockSpec(memory_space=pltpu.HBM),) * 4,
        scratch_shapes=[pltpu.VMEM((ROWS, HALF), BF16), pltpu.SemaphoreType.DMA((10,))],
        compiler_params=pltpu.CompilerParams(vmem_limit_bytes=16 << 20),
    )(merged, basis, factor)


def body(grad_query, grad_key, error_query, error_key, factor_query, factor_key):
    fq, fk = jnp.swapaxes(factor_query, 1, 2), jnp.swapaxes(factor_key, 1, 2)
    kept = reduce(grad_query, grad_key, error_query, error_key, fq, fk)
    new_eq, new_ek, new_q, new_k = refresh(*kept)
    return new_eq, new_ek, jnp.swapaxes(new_q, 1, 2), jnp.swapaxes(new_k, 1, 2)


def solution(mesh):
    split = P("dp", None, "tensor", None)
    return jax.shard_map(
        body,
        mesh=mesh,
        in_specs=(split, split, split, split, P(), P()),
        out_specs=(split, split, P(), P()),
        check_vma=False,
    )
```

```python
import jax
import jax.numpy as jnp
from jax import lax
from jax.experimental import pallas as pl
from jax.experimental.pallas import tpu as pltpu
from jax.sharding import PartitionSpec as P

F32, BF16 = jnp.float32, jnp.bfloat16
D, RANK = 4608, 64
RQ, RK = 512, 256
ROWS = RQ + RK
LOADS, WIDE = 3, D // 3
HALF = D // 2
PART = HALF // 3
LANES = PART // 2
MESH = pl.DeviceIdType.MESH


def dot(a, b, ca=1, cb=0, precision=None):
    return lax.dot_general(a, b, (((ca,), (cb,)), ((), ())), precision=precision, preferred_element_type=F32)


def at(start, size, unit):
    return pl.ds(pl.multiple_of(start, unit), size)


def factorize(gram, inv):
    lane = lax.broadcasted_iota(jnp.int32, (8, 128), 1)
    row = lax.broadcasted_iota(jnp.int32, (8, 128), 0)
    side = jnp.where(lane >= RANK, RANK, 0)
    for i in range(8):
        inv[8 * i:8 * i + 8, :] = jnp.where(lane - side == row + 8 * i, 1.0, 0.0).astype(F32)

    def column(x, j):
        return jnp.take_along_axis(x, side + j, axis=1, mode="promise_in_bounds")

    def block(b, carry):
        here = at(8 * b, 8, 8)
        g = [gram[here, :]] + [gram[8 * i:8 * i + 8, :] for i in range(8)]
        w = [inv[here, :]] + [inv[8 * i:8 * i + 8, :] for i in range(8)]
        done = [None] * 8
        for t in range(0, 8, 2):
            j = 8 * b + t
            row_g0, row_g1 = (jnp.broadcast_to(g[0][r:r + 1, :], (8, 128)) for r in (t, t + 1))
            row_w0, row_w1 = (jnp.broadcast_to(w[0][r:r + 1, :], (8, 128)) for r in (t, t + 1))
            pivot0, beside, pivot1 = column(row_g0, j), column(row_g0, j + 1), column(row_g1, j + 1)
            inverse0 = 1.0 / pivot0
            ratio = beside * inverse0
            pivot1 = pivot1 - ratio * beside
            inverse1 = 1.0 / pivot1
            row_g1, row_w1 = row_g1 - ratio * row_g0, row_w1 - ratio * row_w0
            done[t], done[t + 1] = row_w0 * lax.rsqrt(pivot0), row_w1 * lax.rsqrt(pivot1)
            scaled_g0, scaled_w0 = row_g0 * inverse0, row_w0 * inverse0
            scaled_g1, scaled_w1 = row_g1 * inverse1, row_w1 * inverse1
            for i in range(9):
                c0, c1 = column(g[i], j), column(g[i], j + 1)
                c1 = c1 - ratio * c0
                c0 = jnp.where(row > t if i == 0 else i - 1 > b, c0, 0.0)
                c1 = jnp.where(row > t + 1 if i == 0 else i - 1 > b, c1, 0.0)
                g[i] = g[i] - c0 * scaled_g0 - c1 * scaled_g1
                w[i] = w[i] - c0 * scaled_w0 - c1 * scaled_w1
        last = done[0]
        for t in range(1, 8):
            last = jnp.where(row == t, done[t], last)
        for i in range(8):
            gram[8 * i:8 * i + 8, :] = g[i + 1]
            inv[8 * i:8 * i + 8, :] = w[i + 1]
        inv[here, :] = last
        return carry

    lax.fori_loop(0, 8, block, 0)


def subtract(source, target, basis, factor, start, into):
    cols, there = at(start, PART, 128), at(into, PART, 128)
    for side, rows in ((0, slice(0, RQ)), (1, slice(RQ, ROWS))):
        approx = dot(basis[rows, :], factor[64 * side:64 * side + 64, cols])
        target[rows, there] = (source[rows, cols].astype(F32) - approx).astype(BF16)


def reduce_kernel(gq, gk, eq, ek, fq, fk, merged, basis, factor,
                  psum, inv, white, ebuf, fbuf, ar1, ar2, image_t, image_h,
                  gsend, gsib, gx, psend, psib, pown, rs, ar3,
                  lsem, fsem, s_ar1, r_ar1, s_ar2, r_ar2, s_g, r_g, s_gx, r_gx,
                  s_p, r_p, s_rs, r_rs, s_a3, r_a3, s_ag, r_ag, s_fw, r_fw):
    dp, tensor = lax.axis_index("dp"), lax.axis_index("tensor")
    z, y = lax.div(dp, 4), lax.rem(dp, 4)
    x, c = lax.div(tensor, 2), lax.rem(tensor, 2)

    def device(dz=0, dy=0, dx=0, dc=0):
        return (lax.rem(z + dz, 4) * 4 + lax.rem(y + dy, 4), lax.rem(x + dx, 4) * 2 + lax.rem(c + dc, 2))

    def send(src, dst, ssem, rsem, to):
        pltpu.make_async_remote_copy(src, dst, ssem, rsem, device_id=to, device_id_type=MESH).start()

    def arrived(ref, rsem, ssem):
        pltpu.make_async_remote_copy(ref, ref, ssem, rsem, device_id=device(dc=1), device_id_type=MESH).wait_recv()

    def sent(ref, rsem, ssem):
        pltpu.make_async_remote_copy(ref, ref, ssem, rsem, device_id=device(dc=1), device_id_type=MESH).wait_send()

    loads = [
        pltpu.make_async_copy(fq.at[0], fbuf.at[0], fsem),
        pltpu.make_async_copy(fk.at[0], fbuf.at[1], fsem),
    ]
    for cp in loads:
        cp.start()

    def load(k):
        cols = at(k * WIDE, WIDE, 128)
        return [
            pltpu.make_async_copy(gq.at[0, 0, :, cols], merged.at[0:RQ, cols], lsem.at[k]),
            pltpu.make_async_copy(eq.at[0, 0, :, cols], ebuf.at[0:RQ, cols], lsem.at[k]),
            pltpu.make_async_copy(gk.at[0, 0, :, cols], merged.at[RQ:ROWS, cols], lsem.at[k]),
            pltpu.make_async_copy(ek.at[0, 0, :, cols], ebuf.at[RQ:ROWS, cols], lsem.at[k]),
        ]

    for k in range(LOADS):
        for cp in load(k):
            cp.start()

    offsets = [(a, b, d) for a in range(4) for b in range(4) for d in range(4) if (a, b, d) != (0, 0, 0) and 0 in (a, b, d)]
    barrier = pltpu.get_barrier_semaphore()
    peers = [device(a, b, d) for a, b, d in offsets] + [device(dc=1)]
    for to in peers:
        pl.semaphore_signal(barrier, 1, device_id=to, device_id_type=MESH)

    image_t[...] = jnp.zeros_like(image_t)
    for cp in loads:
        cp.wait()

    def merge(k, carry):
        cols = at(k * WIDE, WIDE, 128)
        for cp in load(k):
            cp.wait()
        merged[:, cols] = (merged[:, cols].astype(F32) + ebuf[:, cols].astype(F32)).astype(BF16)
        image_t[:, 0:RQ] += dot(fbuf[0, :, cols], merged[0:RQ, cols], 1, 1)
        image_t[:, RQ:ROWS] += dot(fbuf[1, :, cols], merged[RQ:ROWS, cols], 1, 1)
        return carry

    lax.fori_loop(0, LOADS, merge, 0)

    pl.semaphore_wait(barrier, len(peers))
    pieces = [(p, p % 2) for p in range(4)]
    first, second = (z, y), (y, z)

    def to(h, d):
        return device(dz=d) if h == 0 else device(dy=d)

    for p, h in pieces:
        mine = ar1.at[p, first[h]]
        mine[...] = image_t[16 * p:16 * p + 16, :].astype(BF16)
        for d in (2, 1, 3):
            send(mine, mine, s_ar1.at[p], r_ar1.at[p], to(h, d))
    for p, h in pieces:
        arrived(ar1.at[p, 0:3], r_ar1.at[p], s_ar1.at[p])
        total = ar1[p, 0].astype(F32)
        for s in (1, 2, 3):
            total += ar1[p, s].astype(F32)
        mine = ar2.at[p, second[h]]
        mine[...] = total.astype(BF16)
        for d in (2, 1, 3):
            send(mine, mine, s_ar2.at[p], r_ar2.at[p], to(1 - h, d))
    for p, h in pieces:
        arrived(ar2.at[p, 0:3], r_ar2.at[p], s_ar2.at[p])
        total = ar2[p, 0].astype(F32)
        for s in (1, 2, 3):
            total += ar2[p, s].astype(F32)
        image_t[16 * p:16 * p + 16, :] = total

    image_h[0:64, :] = image_t[...].astype(BF16)
    image_h[64:128, :] = (image_t[...] - image_h[0:64, :].astype(F32)).astype(BF16)

    def project(start, width=PART):
        cols = at(start, width, 128)
        q = dot(image_h[:, 0:RQ], merged[0:RQ, cols])
        k = dot(image_h[:, RQ:ROWS], merged[RQ:ROWS, cols])
        return q[0:64] + q[64:128], k[0:64] + k[64:128]

    def split(k):
        first, last = lax.div(2 - k, 2), lax.div(k, 2)
        return first, 1 - first - last, last

    def place(k):
        first, middle, last = split(k)
        return z * (1 - last) + y * last, y * first + x * (1 - first), x * first + y * middle + z * last

    def move(k, da, db):
        first, middle, last = split(k)
        return device(da * (1 - last), db * first + da * last, db * (1 - first))

    def along(k, d):
        first, middle, last = split(k)
        return device(d * last, d * middle, d * first)

    def slice_of(a, b):
        return at(16 * (2 * a + lax.div(b, 2)), 16, 16), LANES * lax.rem(b, 2)

    around = [(da, db) for da in range(4) for db in range(4) if (da, db) != (0, 0)]
    around.sort(key=lambda o: -(min(o[0], 4 - o[0]) + min(o[1], 4 - o[1])))

    q, kk = project((1 - c) * HALF, HALF)
    for n in range(3):
        psend[n, 0:64, :] = q[:, PART * n:PART * n + PART].astype(BF16)
        psend[n, 64:128, :] = kk[:, PART * n:PART * n + PART].astype(BF16)
        send(psend.at[n], psib.at[n], s_p.at[n], r_p.at[n], device(dc=1))

    def share(k, carry):
        q, kk = project(c * HALF + PART * k)
        arrived(psib.at[k], r_p.at[k], s_p.at[k])
        pown[k, 0:64, :] = (q + psib[k, 0:64, :].astype(F32)).astype(BF16)
        pown[k, 64:128, :] = (kk + psib[k, 64:128, :].astype(F32)).astype(BF16)
        a, b, _ = place(k)
        for da, db in around:
            rows, lanes = slice_of(lax.rem(a + da, 4), lax.rem(b + db, 4))
            send(pown.at[k, rows, at(lanes, LANES, 128)], rs.at[k, 4 * a + b], s_rs.at[k], r_rs.at[k], move(k, da, db))
        rows, lanes = slice_of(a, b)
        rs[k, 4 * a + b] = pown[k, rows, at(lanes, LANES, 128)]

        return carry

    lax.fori_loop(0, 3, share, 0)

    high = lax.Precision.HIGHEST
    tq, tk = image_t[:, 0:RQ], image_t[:, RQ:ROWS]
    gsend[...] = jnp.concatenate([dot(tq, tq, 1, 1, high), dot(tk, tk, 1, 1, high)], axis=1)
    send(gsend, gsib, s_g, r_g, device(dc=1))
    arrived(gsib, r_g, s_g)
    gx[x] = gsend[...] + gsib[...]
    for d in (2, 1, 3):
        send(gx.at[x], gx.at[x], s_gx, r_gx, device(dx=d))

    def gather(k, carry):
        arrived(rs.at[k, 0:15], r_rs.at[k], s_rs.at[k])
        total = rs[k, 0].astype(F32)
        for s in range(1, 16):
            total += rs[k, s].astype(F32)
        m = place(k)[2]
        ar3[k, m] = total.astype(BF16)
        for d in (2, 1, 3):
            send(ar3.at[k, m], ar3.at[k, m], s_a3.at[k], r_a3.at[k], along(k, d))
        return carry

    lax.fori_loop(0, 3, gather, 0)

    def spread(k, carry):
        arrived(ar3.at[k, 0:3], r_a3.at[k], s_a3.at[k])
        total = ar3[k, 0].astype(F32)
        for s in (1, 2, 3):
            total += ar3[k, s].astype(F32)
        a, b, _ = place(k)
        rows, lanes = slice_of(a, b)
        spot = (rows, at(c * HALF + PART * k + lanes, LANES, 128))
        psum[spot] = total.astype(BF16)
        for da, db in around:
            send(psum.at[spot], psum.at[spot], s_ag.at[k], r_ag.at[k], move(k, da, db))
        return carry

    lax.fori_loop(0, 3, spread, 0)

    arrived(gx.at[0:3], r_gx, s_gx)
    gsib[...] = (gx[0] + gx[1]) + (gx[2] + gx[3])
    factorize(gsib, inv)
    both = inv[...]
    for side, rows in ((0, slice(0, RQ)), (1, slice(RQ, ROWS))):
        w = both[:, 64 * side:64 * side + 64]
        basis[rows, :] = dot(image_t[:, rows], w, 0, 1, high).astype(BF16) * 0.0625
        hi = w.astype(BF16)
        white[side, 0:64] = hi
        white[side, 64:128] = (w - hi.astype(F32)).astype(BF16)

    def whiten(k, carry):
        arrived(rs.at[k, 0:15], r_ag.at[k], s_ag.at[k])
        cols = at(c * HALF + PART * k, PART, 128)
        for side in (0, 1):
            f = dot(white[side], psum[64 * side:64 * side + 64, cols])
            factor[64 * side:64 * side + 64, cols] = (f[0:64] + f[64:128]).astype(BF16)
        send(factor.at[:, cols], factor.at[:, cols], s_fw.at[k], r_fw.at[k], device(dc=1))
        return carry

    lax.fori_loop(0, 3, whiten, 0)

    def errors(k, carry):
        start = c * HALF + PART * k
        subtract(merged, merged, basis, factor, start, start)
        return carry

    lax.fori_loop(0, 3, errors, 0)

    sent(gsend, r_g, s_g)
    sent(gx.at[0:3], r_gx, s_gx)
    for p in range(4):
        sent(ar1.at[p, 0:3], r_ar1.at[p], s_ar1.at[p])
        sent(ar2.at[p, 0:3], r_ar2.at[p], s_ar2.at[p])
    for k in range(3):
        sent(psend.at[k], r_p.at[k], s_p.at[k])
        sent(rs.at[k, 0:15], r_rs.at[k], s_rs.at[k])
        sent(ar3.at[k, 0:3], r_a3.at[k], s_a3.at[k])
        sent(rs.at[k, 0:15], r_ag.at[k], s_ag.at[k])
    for k in range(3):
        arrived(psend.at[k], r_fw.at[k], s_fw.at[k])
        sent(psend.at[k], r_fw.at[k], s_fw.at[k])


def reduce(gq, gk, eq, ek, fq, fk):
    dma, vmem = pltpu.SemaphoreType.DMA, pltpu.VMEM
    return pl.pallas_call(
        reduce_kernel,
        name="reduce",
        out_shape=(
            vmem((ROWS, D), BF16),
            vmem((ROWS, RANK), BF16),
            vmem((2 * RANK, D), BF16),
        ),
        in_specs=[pl.BlockSpec(memory_space=pltpu.HBM)] * 6,
        out_specs=(pl.BlockSpec(memory_space=vmem),) * 3,
        scratch_shapes=[
            vmem((2 * RANK, D), BF16),
            vmem((RANK, 128), F32),
            vmem((2, 128, RANK), BF16),
            vmem((ROWS, D), BF16),
            vmem((2, RANK, D), BF16),
            vmem((4, 4, 16, ROWS), BF16),
            vmem((4, 4, 16, ROWS), BF16),
            vmem((RANK, ROWS), F32),
            vmem((2 * RANK, ROWS), BF16),
            vmem((RANK, 128), F32),
            vmem((RANK, 128), F32),
            vmem((4, RANK, 128), F32),
            vmem((3, 128, PART), BF16),
            vmem((3, 128, PART), BF16),
            vmem((3, 128, PART), BF16),
            vmem((3, 16, 16, LANES), BF16),
            vmem((3, 4, 16, LANES), BF16),
            dma((LOADS,)), dma,
            dma((4,)), dma((4,)), dma((4,)), dma((4,)),
            dma, dma, dma, dma,
            dma((3,)), dma((3,)), dma((3,)), dma((3,)), dma((3,)), dma((3,)),
            dma((3,)), dma((3,)), dma((3,)), dma((3,)),
        ],
        compiler_params=pltpu.CompilerParams(
            collective_id=0, has_side_effects=True, vmem_limit_bytes=53 << 20
        ),
    )(gq, gk, eq, ek, fq, fk)


def refresh_kernel(merged, basis, factor, error_q, error_k, new_q, new_k, buf, sem):
    c = lax.rem(lax.axis_index("tensor"), 2)
    own, other = c * HALF, (1 - c) * HALF
    mine = at(own, HALF, 128)
    copies = [
        pltpu.make_async_copy(merged.at[0:RQ, mine], error_q.at[0, 0, :, mine], sem.at[0]),
        pltpu.make_async_copy(merged.at[RQ:ROWS, mine], error_k.at[0, 0, :, mine], sem.at[1]),
        pltpu.make_async_copy(factor.at[0:RANK], new_q.at[0], sem.at[2]),
        pltpu.make_async_copy(factor.at[RANK:2 * RANK], new_k.at[0], sem.at[3]),
    ]
    for cp in copies:
        cp.start()
    def part(k):
        here, there = at(PART * k, PART, 128), at(other + PART * k, PART, 128)
        return [
            pltpu.make_async_copy(buf.at[0:RQ, here], error_q.at[0, 0, :, there], sem.at[4 + 2 * k]),
            pltpu.make_async_copy(buf.at[RQ:ROWS, here], error_k.at[0, 0, :, there], sem.at[5 + 2 * k]),
        ]

    def errors(k, carry):
        subtract(merged, buf, basis, factor, other + PART * k, PART * k)
        for cp in part(k):
            cp.start()
        return carry

    lax.fori_loop(0, 3, errors, 0)
    for k in range(3):
        copies += part(k)
    for cp in copies:
        cp.wait()


def refresh(merged, basis, factor):
    return pl.pallas_call(
        refresh_kernel,
        name="refresh",
        out_shape=(
            jax.ShapeDtypeStruct((1, 1, RQ, D), BF16),
            jax.ShapeDtypeStruct((1, 1, RK, D), BF16),
            jax.ShapeDtypeStruct((1, RANK, D), BF16),
            jax.ShapeDtypeStruct((1, RANK, D), BF16),
        ),
        in_specs=[pl.BlockSpec(memory_space=pltpu.VMEM)] * 3,
        out_specs=(pl.BlockSpec(memory_space=pltpu.HBM),) * 4,
        scratch_shapes=[pltpu.VMEM((ROWS, HALF), BF16), pltpu.SemaphoreType.DMA((10,))],
        compiler_params=pltpu.CompilerParams(vmem_limit_bytes=16 << 20),
    )(merged, basis, factor)


def body(grad_query, grad_key, error_query, error_key, factor_query, factor_key):
    fq, fk = jnp.swapaxes(factor_query, 1, 2), jnp.swapaxes(factor_key, 1, 2)
    kept = reduce(grad_query, grad_key, error_query, error_key, fq, fk)
    new_eq, new_ek, new_q, new_k = refresh(*kept)
    return new_eq, new_ek, jnp.swapaxes(new_q, 1, 2), jnp.swapaxes(new_k, 1, 2)


def solution(mesh):
    split = P("dp", None, "tensor", None)
    return jax.shard_map(
        body,
        mesh=mesh,
        in_specs=(split, split, split, split, P(), P()),
        out_specs=(split, split, P(), P()),
        check_vma=False,
    )
```

```python
import jax
import jax.numpy as jnp
from jax import lax
from jax.experimental import pallas as pl
from jax.experimental.pallas import tpu as pltpu
from jax.sharding import PartitionSpec as P

F32, BF16 = jnp.float32, jnp.bfloat16
D, RANK = 4608, 64
RQ, RK = 512, 256
ROWS = RQ + RK
BLOCK = 256
BLOCKS = ROWS // BLOCK
HALF = D // 2
PART = HALF // 3
LANES = PART // 2
MESH = pl.DeviceIdType.MESH


def dot(a, b, ca=1, cb=0, precision=None):
    return lax.dot_general(a, b, (((ca,), (cb,)), ((), ())), precision=precision, preferred_element_type=F32)


def at(start, size, unit):
    return pl.ds(pl.multiple_of(start, unit), size)


def factorize(gram, inv):
    lane = lax.broadcasted_iota(jnp.int32, (8, 128), 1)
    row = lax.broadcasted_iota(jnp.int32, (8, 128), 0)
    side = jnp.where(lane >= RANK, RANK, 0)
    for i in range(8):
        inv[8 * i:8 * i + 8, :] = jnp.where(lane - side == row + 8 * i, 1.0, 0.0).astype(F32)

    def column(x, j):
        return jnp.take_along_axis(x, side + j, axis=1, mode="promise_in_bounds")

    def block(b, carry):
        here = at(8 * b, 8, 8)
        g = [gram[here, :]] + [gram[8 * i:8 * i + 8, :] for i in range(8)]
        w = [inv[here, :]] + [inv[8 * i:8 * i + 8, :] for i in range(8)]
        done = [None] * 8
        for t in range(0, 8, 2):
            j = 8 * b + t
            row_g0, row_g1 = (jnp.broadcast_to(g[0][r:r + 1, :], (8, 128)) for r in (t, t + 1))
            row_w0, row_w1 = (jnp.broadcast_to(w[0][r:r + 1, :], (8, 128)) for r in (t, t + 1))
            pivot0, beside, pivot1 = column(row_g0, j), column(row_g0, j + 1), column(row_g1, j + 1)
            inverse0 = 1.0 / pivot0
            ratio = beside * inverse0
            pivot1 = pivot1 - ratio * beside
            inverse1 = 1.0 / pivot1
            row_g1, row_w1 = row_g1 - ratio * row_g0, row_w1 - ratio * row_w0
            done[t], done[t + 1] = row_w0 * lax.rsqrt(pivot0), row_w1 * lax.rsqrt(pivot1)
            scaled_g0, scaled_w0 = row_g0 * inverse0, row_w0 * inverse0
            scaled_g1, scaled_w1 = row_g1 * inverse1, row_w1 * inverse1
            for i in range(9):
                c0, c1 = column(g[i], j), column(g[i], j + 1)
                c1 = c1 - ratio * c0
                c0 = jnp.where(row > t if i == 0 else i - 1 > b, c0, 0.0)
                c1 = jnp.where(row > t + 1 if i == 0 else i - 1 > b, c1, 0.0)
                g[i] = g[i] - c0 * scaled_g0 - c1 * scaled_g1
                w[i] = w[i] - c0 * scaled_w0 - c1 * scaled_w1
        last = done[0]
        for t in range(1, 8):
            last = jnp.where(row == t, done[t], last)
        for i in range(8):
            gram[8 * i:8 * i + 8, :] = g[i + 1]
            inv[8 * i:8 * i + 8, :] = w[i + 1]
        inv[here, :] = last
        return carry

    lax.fori_loop(0, 8, block, 0)


def subtract(source, target, basis, factor, start, into):
    cols, there = at(start, PART, 128), at(into, PART, 128)
    for side, rows in ((0, slice(0, RQ)), (1, slice(RQ, ROWS))):
        approx = dot(basis[rows, :], factor[64 * side:64 * side + 64, cols])
        target[rows, there] = (source[rows, cols].astype(F32) - approx).astype(BF16)


def reduce_kernel(gq, gk, eq, ek, fq, fk, merged, basis, factor,
                  psum, inv, white, ebuf, fbuf, ar1, ar2, image_t, image_h,
                  gsend, gsib, gx, psend, psib, pown, rs, ar3,
                  lsem, fsem, s_ar1, r_ar1, s_ar2, r_ar2, s_g, r_g, s_gx, r_gx,
                  s_p, r_p, s_rs, r_rs, s_a3, r_a3, s_ag, r_ag, s_fw, r_fw):
    dp, tensor = lax.axis_index("dp"), lax.axis_index("tensor")
    z, y = lax.div(dp, 4), lax.rem(dp, 4)
    x, c = lax.div(tensor, 2), lax.rem(tensor, 2)

    def device(dz=0, dy=0, dx=0, dc=0):
        return (lax.rem(z + dz, 4) * 4 + lax.rem(y + dy, 4), lax.rem(x + dx, 4) * 2 + lax.rem(c + dc, 2))

    def send(src, dst, ssem, rsem, to):
        pltpu.make_async_remote_copy(src, dst, ssem, rsem, device_id=to, device_id_type=MESH).start()

    def arrived(ref, rsem, ssem):
        pltpu.make_async_remote_copy(ref, ref, ssem, rsem, device_id=device(dc=1), device_id_type=MESH).wait_recv()

    def sent(ref, rsem, ssem):
        pltpu.make_async_remote_copy(ref, ref, ssem, rsem, device_id=device(dc=1), device_id_type=MESH).wait_send()

    loads = [
        pltpu.make_async_copy(fq.at[0], fbuf.at[0], fsem),
        pltpu.make_async_copy(fk.at[0], fbuf.at[1], fsem),
    ]
    for cp in loads:
        cp.start()

    for k, (grad, error, row) in enumerate(((gq, eq, 0), (gq, eq, BLOCK), (gk, ek, 0))):
        rows, there = pl.ds(row, BLOCK), pl.ds(BLOCK * k, BLOCK)
        pltpu.make_async_copy(grad.at[0, 0, rows], merged.at[there], lsem.at[k]).start()
        pltpu.make_async_copy(error.at[0, 0, rows], ebuf.at[there], lsem.at[k]).start()

    offsets = [(a, b, d) for a in range(4) for b in range(4) for d in range(4) if (a, b, d) != (0, 0, 0) and 0 in (a, b, d)]
    barrier = pltpu.get_barrier_semaphore()
    peers = [device(a, b, d) for a, b, d in offsets] + [device(dc=1)]
    for to in peers:
        pl.semaphore_signal(barrier, 1, device_id=to, device_id_type=MESH)

    first, second = (z, y), (y, z)

    def to(h, d):
        return device(dz=d) if h == 0 else device(dy=d)

    for cp in loads:
        cp.wait()

    def merge(k, carry):
        rows = at(BLOCK * k, BLOCK, BLOCK)
        pltpu.make_async_copy(gk.at[0, 0], merged.at[rows], lsem.at[k]).wait()
        pltpu.make_async_copy(ek.at[0, 0], ebuf.at[rows], lsem.at[k]).wait()
        merged[rows, :] = (merged[rows, :].astype(F32) + ebuf[rows, :].astype(F32)).astype(BF16)
        part = dot(fbuf[lax.div(k, 2)], merged[rows, :], 1, 1)

        @pl.when(k == 0)
        def _():
            pl.semaphore_wait(barrier, len(peers))

        for h in (0, 1):
            mine = ar1.at[k, h, first[h]]
            mine[...] = part[32 * h:32 * h + 32].astype(BF16)
            for d in (2, 1, 3):
                send(mine, mine, s_ar1.at[k, h], r_ar1.at[k, h], to(h, d))
        return carry

    lax.fori_loop(0, BLOCKS, merge, 0)

    def relay(k, carry):
        for h in (0, 1):
            arrived(ar1.at[k, h, 0:3], r_ar1.at[k, h], s_ar1.at[k, h])
            total = ar1[k, h, 0].astype(F32)
            for s in (1, 2, 3):
                total += ar1[k, h, s].astype(F32)
            mine = ar2.at[k, h, second[h]]
            mine[...] = total.astype(BF16)
            for d in (2, 1, 3):
                send(mine, mine, s_ar2.at[k, h], r_ar2.at[k, h], to(1 - h, d))
        return carry

    lax.fori_loop(0, BLOCKS, relay, 0)

    def finish(k, carry):
        for h in (0, 1):
            arrived(ar2.at[k, h, 0:3], r_ar2.at[k, h], s_ar2.at[k, h])
            total = ar2[k, h, 0].astype(F32)
            for s in (1, 2, 3):
                total += ar2[k, h, s].astype(F32)
            image_t[32 * h:32 * h + 32, at(BLOCK * k, BLOCK, BLOCK)] = total
        return carry

    lax.fori_loop(0, BLOCKS, finish, 0)

    image_h[0:64, :] = image_t[...].astype(BF16)
    image_h[64:128, :] = (image_t[...] - image_h[0:64, :].astype(F32)).astype(BF16)

    def project(start, width=PART):
        cols = at(start, width, 128)
        q = dot(image_h[:, 0:RQ], merged[0:RQ, cols])
        k = dot(image_h[:, RQ:ROWS], merged[RQ:ROWS, cols])
        return q[0:64] + q[64:128], k[0:64] + k[64:128]

    def split(k):
        first, last = lax.div(2 - k, 2), lax.div(k, 2)
        return first, 1 - first - last, last

    def place(k):
        first, middle, last = split(k)
        return z * (1 - last) + y * last, y * first + x * (1 - first), x * first + y * middle + z * last

    def move(k, da, db):
        first, middle, last = split(k)
        return device(da * (1 - last), db * first + da * last, db * (1 - first))

    def along(k, d):
        first, middle, last = split(k)
        return device(d * last, d * middle, d * first)

    def slice_of(a, b):
        return at(16 * (2 * a + lax.div(b, 2)), 16, 16), LANES * lax.rem(b, 2)

    around = [(da, db) for da in range(4) for db in range(4) if (da, db) != (0, 0)]
    around.sort(key=lambda o: -(min(o[0], 4 - o[0]) + min(o[1], 4 - o[1])))

    q, kk = project((1 - c) * HALF, HALF)
    for n in range(3):
        psend[n, 0:64, :] = q[:, PART * n:PART * n + PART].astype(BF16)
        psend[n, 64:128, :] = kk[:, PART * n:PART * n + PART].astype(BF16)
        send(psend.at[n], psib.at[n], s_p.at[n], r_p.at[n], device(dc=1))

    def share(k, carry):
        q, kk = project(c * HALF + PART * k)
        arrived(psib.at[k], r_p.at[k], s_p.at[k])
        pown[k, 0:64, :] = (q + psib[k, 0:64, :].astype(F32)).astype(BF16)
        pown[k, 64:128, :] = (kk + psib[k, 64:128, :].astype(F32)).astype(BF16)
        a, b, _ = place(k)
        for da, db in around:
            rows, lanes = slice_of(lax.rem(a + da, 4), lax.rem(b + db, 4))
            send(pown.at[k, rows, at(lanes, LANES, 128)], rs.at[k, 4 * a + b], s_rs.at[k], r_rs.at[k], move(k, da, db))
        rows, lanes = slice_of(a, b)
        rs[k, 4 * a + b] = pown[k, rows, at(lanes, LANES, 128)]

        return carry

    lax.fori_loop(0, 3, share, 0)

    high = lax.Precision.HIGHEST
    tq, tk = image_t[:, 0:RQ], image_t[:, RQ:ROWS]
    gsend[...] = jnp.concatenate([dot(tq, tq, 1, 1, high), dot(tk, tk, 1, 1, high)], axis=1)
    send(gsend, gsib, s_g, r_g, device(dc=1))
    arrived(gsib, r_g, s_g)
    gx[x] = gsend[...] + gsib[...]
    for d in (2, 1, 3):
        send(gx.at[x], gx.at[x], s_gx, r_gx, device(dx=d))

    def gather(k, carry):
        arrived(rs.at[k, 0:15], r_rs.at[k], s_rs.at[k])
        total = rs[k, 0].astype(F32)
        for s in range(1, 16):
            total += rs[k, s].astype(F32)
        m = place(k)[2]
        ar3[k, m] = total.astype(BF16)
        for d in (2, 1, 3):
            send(ar3.at[k, m], ar3.at[k, m], s_a3.at[k], r_a3.at[k], along(k, d))
        return carry

    lax.fori_loop(0, 3, gather, 0)

    def spread(k, carry):
        arrived(ar3.at[k, 0:3], r_a3.at[k], s_a3.at[k])
        total = ar3[k, 0].astype(F32)
        for s in (1, 2, 3):
            total += ar3[k, s].astype(F32)
        a, b, _ = place(k)
        rows, lanes = slice_of(a, b)
        spot = (rows, at(c * HALF + PART * k + lanes, LANES, 128))
        psum[spot] = total.astype(BF16)
        for da, db in around:
            send(psum.at[spot], psum.at[spot], s_ag.at[k], r_ag.at[k], move(k, da, db))
        return carry

    lax.fori_loop(0, 3, spread, 0)

    arrived(gx.at[0:3], r_gx, s_gx)
    gsib[...] = (gx[0] + gx[1]) + (gx[2] + gx[3])
    factorize(gsib, inv)
    both = inv[...]
    for side, rows in ((0, slice(0, RQ)), (1, slice(RQ, ROWS))):
        w = both[:, 64 * side:64 * side + 64]
        basis[rows, :] = dot(image_t[:, rows], w, 0, 1, high).astype(BF16) * 0.0625
        hi = w.astype(BF16)
        white[side, 0:64] = hi
        white[side, 64:128] = (w - hi.astype(F32)).astype(BF16)

    def whiten(k, carry):
        arrived(rs.at[k, 0:15], r_ag.at[k], s_ag.at[k])
        cols = at(c * HALF + PART * k, PART, 128)
        for side in (0, 1):
            f = dot(white[side], psum[64 * side:64 * side + 64, cols])
            factor[64 * side:64 * side + 64, cols] = (f[0:64] + f[64:128]).astype(BF16)
        send(factor.at[:, cols], factor.at[:, cols], s_fw.at[k], r_fw.at[k], device(dc=1))
        return carry

    lax.fori_loop(0, 3, whiten, 0)

    def errors(k, carry):
        start = c * HALF + PART * k
        subtract(merged, merged, basis, factor, start, start)
        return carry

    lax.fori_loop(0, 3, errors, 0)

    sent(gsend, r_g, s_g)
    sent(gx.at[0:3], r_gx, s_gx)
    for k in range(BLOCKS):
        for h in (0, 1):
            sent(ar1.at[k, h, 0:3], r_ar1.at[k, h], s_ar1.at[k, h])
            sent(ar2.at[k, h, 0:3], r_ar2.at[k, h], s_ar2.at[k, h])
    for k in range(3):
        sent(psend.at[k], r_p.at[k], s_p.at[k])
        sent(rs.at[k, 0:15], r_rs.at[k], s_rs.at[k])
        sent(ar3.at[k, 0:3], r_a3.at[k], s_a3.at[k])
        sent(rs.at[k, 0:15], r_ag.at[k], s_ag.at[k])
    for k in range(3):
        arrived(psend.at[k], r_fw.at[k], s_fw.at[k])
        sent(psend.at[k], r_fw.at[k], s_fw.at[k])


def reduce(gq, gk, eq, ek, fq, fk):
    dma, vmem = pltpu.SemaphoreType.DMA, pltpu.VMEM
    return pl.pallas_call(
        reduce_kernel,
        name="reduce",
        out_shape=(
            vmem((ROWS, D), BF16),
            vmem((ROWS, RANK), BF16),
            vmem((2 * RANK, D), BF16),
        ),
        in_specs=[pl.BlockSpec(memory_space=pltpu.HBM)] * 6,
        out_specs=(pl.BlockSpec(memory_space=vmem),) * 3,
        scratch_shapes=[
            vmem((2 * RANK, D), BF16),
            vmem((RANK, 128), F32),
            vmem((2, 128, RANK), BF16),
            vmem((ROWS, D), BF16),
            vmem((2, RANK, D), BF16),
            vmem((BLOCKS, 2, 4, 32, BLOCK), BF16),
            vmem((BLOCKS, 2, 4, 32, BLOCK), BF16),
            vmem((RANK, ROWS), F32),
            vmem((2 * RANK, ROWS), BF16),
            vmem((RANK, 128), F32),
            vmem((RANK, 128), F32),
            vmem((4, RANK, 128), F32),
            vmem((3, 128, PART), BF16),
            vmem((3, 128, PART), BF16),
            vmem((3, 128, PART), BF16),
            vmem((3, 16, 16, LANES), BF16),
            vmem((3, 4, 16, LANES), BF16),
            dma((BLOCKS,)), dma,
            dma((BLOCKS, 2)), dma((BLOCKS, 2)), dma((BLOCKS, 2)), dma((BLOCKS, 2)),
            dma, dma, dma, dma,
            dma((3,)), dma((3,)), dma((3,)), dma((3,)), dma((3,)), dma((3,)),
            dma((3,)), dma((3,)), dma((3,)), dma((3,)),
        ],
        compiler_params=pltpu.CompilerParams(
            collective_id=0, has_side_effects=True, vmem_limit_bytes=53 << 20
        ),
    )(gq, gk, eq, ek, fq, fk)


def refresh_kernel(merged, basis, factor, error_q, error_k, new_q, new_k, buf, sem):
    c = lax.rem(lax.axis_index("tensor"), 2)
    own, other = c * HALF, (1 - c) * HALF
    mine = at(own, HALF, 128)
    copies = [
        pltpu.make_async_copy(merged.at[0:RQ, mine], error_q.at[0, 0, :, mine], sem.at[0]),
        pltpu.make_async_copy(merged.at[RQ:ROWS, mine], error_k.at[0, 0, :, mine], sem.at[1]),
        pltpu.make_async_copy(factor.at[0:RANK], new_q.at[0], sem.at[2]),
        pltpu.make_async_copy(factor.at[RANK:2 * RANK], new_k.at[0], sem.at[3]),
    ]
    for cp in copies:
        cp.start()
    def part(k):
        here, there = at(PART * k, PART, 128), at(other + PART * k, PART, 128)
        return [
            pltpu.make_async_copy(buf.at[0:RQ, here], error_q.at[0, 0, :, there], sem.at[4 + 2 * k]),
            pltpu.make_async_copy(buf.at[RQ:ROWS, here], error_k.at[0, 0, :, there], sem.at[5 + 2 * k]),
        ]

    def errors(k, carry):
        subtract(merged, buf, basis, factor, other + PART * k, PART * k)
        for cp in part(k):
            cp.start()
        return carry

    lax.fori_loop(0, 3, errors, 0)
    for k in range(3):
        copies += part(k)
    for cp in copies:
        cp.wait()


def refresh(merged, basis, factor):
    return pl.pallas_call(
        refresh_kernel,
        name="refresh",
        out_shape=(
            jax.ShapeDtypeStruct((1, 1, RQ, D), BF16),
            jax.ShapeDtypeStruct((1, 1, RK, D), BF16),
            jax.ShapeDtypeStruct((1, RANK, D), BF16),
            jax.ShapeDtypeStruct((1, RANK, D), BF16),
        ),
        in_specs=[pl.BlockSpec(memory_space=pltpu.VMEM)] * 3,
        out_specs=(pl.BlockSpec(memory_space=pltpu.HBM),) * 4,
        scratch_shapes=[pltpu.VMEM((ROWS, HALF), BF16), pltpu.SemaphoreType.DMA((10,))],
        compiler_params=pltpu.CompilerParams(vmem_limit_bytes=16 << 20),
    )(merged, basis, factor)


def body(grad_query, grad_key, error_query, error_key, factor_query, factor_key):
    fq, fk = jnp.swapaxes(factor_query, 1, 2), jnp.swapaxes(factor_key, 1, 2)
    kept = reduce(grad_query, grad_key, error_query, error_key, fq, fk)
    new_eq, new_ek, new_q, new_k = refresh(*kept)
    return new_eq, new_ek, jnp.swapaxes(new_q, 1, 2), jnp.swapaxes(new_k, 1, 2)


def solution(mesh):
    split = P("dp", None, "tensor", None)
    return jax.shard_map(
        body,
        mesh=mesh,
        in_specs=(split, split, split, split, P(), P()),
        out_specs=(split, split, P(), P()),
        check_vma=False,
    )
```

```python
import jax
import jax.numpy as jnp
from jax import lax
from jax.experimental import pallas as pl
from jax.experimental.pallas import tpu as pltpu
from jax.sharding import PartitionSpec as P

F32, BF16 = jnp.float32, jnp.bfloat16
D, RANK = 4608, 64
RQ, RK = 512, 256
ROWS = RQ + RK
BLOCK = 256
BLOCKS = ROWS // BLOCK
HALF = D // 2
PART = HALF // 3
LANES = PART // 2
MESH = pl.DeviceIdType.MESH


def dot(a, b, ca=1, cb=0, precision=None):
    return lax.dot_general(a, b, (((ca,), (cb,)), ((), ())), precision=precision, preferred_element_type=F32)


def at(start, size, unit):
    return pl.ds(pl.multiple_of(start, unit), size)


def factorize(gram, inv):
    lane = lax.broadcasted_iota(jnp.int32, (8, 128), 1)
    row = lax.broadcasted_iota(jnp.int32, (8, 128), 0)
    side = jnp.where(lane >= RANK, RANK, 0)
    for i in range(8):
        inv[8 * i:8 * i + 8, :] = jnp.where(lane - side == row + 8 * i, 1.0, 0.0).astype(F32)

    def column(x, j):
        return jnp.take_along_axis(x, side + j, axis=1, mode="promise_in_bounds")

    def block(b, carry):
        here = at(8 * b, 8, 8)
        g = [gram[here, :]] + [gram[8 * i:8 * i + 8, :] for i in range(8)]
        w = [inv[here, :]] + [inv[8 * i:8 * i + 8, :] for i in range(8)]
        done = [None] * 8
        for t in range(0, 8, 2):
            j = 8 * b + t
            row_g0, row_g1 = (jnp.broadcast_to(g[0][r:r + 1, :], (8, 128)) for r in (t, t + 1))
            row_w0, row_w1 = (jnp.broadcast_to(w[0][r:r + 1, :], (8, 128)) for r in (t, t + 1))
            pivot0, beside, pivot1 = column(row_g0, j), column(row_g0, j + 1), column(row_g1, j + 1)
            inverse0 = 1.0 / pivot0
            ratio = beside * inverse0
            pivot1 = pivot1 - ratio * beside
            inverse1 = 1.0 / pivot1
            row_g1, row_w1 = row_g1 - ratio * row_g0, row_w1 - ratio * row_w0
            done[t], done[t + 1] = row_w0 * lax.rsqrt(pivot0), row_w1 * lax.rsqrt(pivot1)
            scaled_g0, scaled_w0 = row_g0 * inverse0, row_w0 * inverse0
            scaled_g1, scaled_w1 = row_g1 * inverse1, row_w1 * inverse1
            for i in range(9):
                c0, c1 = column(g[i], j), column(g[i], j + 1)
                c1 = c1 - ratio * c0
                c0 = jnp.where(row > t if i == 0 else i - 1 > b, c0, 0.0)
                c1 = jnp.where(row > t + 1 if i == 0 else i - 1 > b, c1, 0.0)
                g[i] = g[i] - c0 * scaled_g0 - c1 * scaled_g1
                w[i] = w[i] - c0 * scaled_w0 - c1 * scaled_w1
        last = done[0]
        for t in range(1, 8):
            last = jnp.where(row == t, done[t], last)
        for i in range(8):
            gram[8 * i:8 * i + 8, :] = g[i + 1]
            inv[8 * i:8 * i + 8, :] = w[i + 1]
        inv[here, :] = last
        return carry

    lax.fori_loop(0, 8, block, 0)


def subtract(source, target, basis, factor, start, into):
    cols, there = at(start, PART, 128), at(into, PART, 128)
    for side, rows in ((0, slice(0, RQ)), (1, slice(RQ, ROWS))):
        approx = dot(basis[rows, :], factor[64 * side:64 * side + 64, cols])
        target[rows, there] = (source[rows, cols].astype(F32) - approx).astype(BF16)


def reduce_kernel(gq, gk, eq, ek, fq, fk, merged, basis, factor,
                  psum, inv, white, ebuf, fbuf, ar1, ar2, image_t, image_h,
                  gsend, gsib, gx, qown, psend, psib, pown, rs, ar3,
                  lsem, fsem, s_ar1, r_ar1, s_ar2, r_ar2, s_g, r_g, s_gx, r_gx,
                  s_p, r_p, s_rs, r_rs, s_a3, r_a3, s_ag, r_ag, s_fw, r_fw):
    dp, tensor = lax.axis_index("dp"), lax.axis_index("tensor")
    z, y = lax.div(dp, 4), lax.rem(dp, 4)
    x, c = lax.div(tensor, 2), lax.rem(tensor, 2)

    def device(dz=0, dy=0, dx=0, dc=0):
        return (lax.rem(z + dz, 4) * 4 + lax.rem(y + dy, 4), lax.rem(x + dx, 4) * 2 + lax.rem(c + dc, 2))

    def send(src, dst, ssem, rsem, to):
        pltpu.make_async_remote_copy(src, dst, ssem, rsem, device_id=to, device_id_type=MESH).start()

    def arrived(ref, rsem, ssem):
        pltpu.make_async_remote_copy(ref, ref, ssem, rsem, device_id=device(dc=1), device_id_type=MESH).wait_recv()

    def sent(ref, rsem, ssem):
        pltpu.make_async_remote_copy(ref, ref, ssem, rsem, device_id=device(dc=1), device_id_type=MESH).wait_send()

    loads = [
        pltpu.make_async_copy(fq.at[0], fbuf.at[0], fsem),
        pltpu.make_async_copy(fk.at[0], fbuf.at[1], fsem),
    ]
    for cp in loads:
        cp.start()

    for k, (grad, error, row) in enumerate(((gq, eq, 0), (gq, eq, BLOCK), (gk, ek, 0))):
        rows, there = pl.ds(row, BLOCK), pl.ds(BLOCK * k, BLOCK)
        pltpu.make_async_copy(grad.at[0, 0, rows], merged.at[there], lsem.at[k]).start()
        pltpu.make_async_copy(error.at[0, 0, rows], ebuf.at[there], lsem.at[k]).start()

    offsets = [(a, b, d) for a in range(4) for b in range(4) for d in range(4) if (a, b, d) != (0, 0, 0) and 0 in (a, b, d)]
    barrier = pltpu.get_barrier_semaphore()
    peers = [device(a, b, d) for a, b, d in offsets] + [device(dc=1)]
    for to in peers:
        pl.semaphore_signal(barrier, 1, device_id=to, device_id_type=MESH)

    first, second = (z, y), (y, z)

    def to(h, d):
        return device(dz=d) if h == 0 else device(dy=d)

    for cp in loads:
        cp.wait()

    def merge(k, carry):
        rows = at(BLOCK * k, BLOCK, BLOCK)
        pltpu.make_async_copy(gk.at[0, 0], merged.at[rows], lsem.at[k]).wait()
        pltpu.make_async_copy(ek.at[0, 0], ebuf.at[rows], lsem.at[k]).wait()
        merged[rows, :] = (merged[rows, :].astype(F32) + ebuf[rows, :].astype(F32)).astype(BF16)
        part = dot(fbuf[lax.div(k, 2)], merged[rows, :], 1, 1)

        @pl.when(k == 0)
        def _():
            pl.semaphore_wait(barrier, len(peers))

        for h in (0, 1):
            mine = ar1.at[k, h, first[h]]
            mine[...] = part[32 * h:32 * h + 32].astype(BF16)
            for d in (2, 1, 3):
                send(mine, mine, s_ar1.at[k, h], r_ar1.at[k, h], to(h, d))
        return carry

    lax.fori_loop(0, BLOCKS, merge, 0)

    def relay(k, carry):
        for h in (0, 1):
            arrived(ar1.at[k, h, 0:3], r_ar1.at[k, h], s_ar1.at[k, h])
            total = ar1[k, h, 0].astype(F32)
            for s in (1, 2, 3):
                total += ar1[k, h, s].astype(F32)
            mine = ar2.at[k, h, second[h]]
            mine[...] = total.astype(BF16)
            for d in (2, 1, 3):
                send(mine, mine, s_ar2.at[k, h], r_ar2.at[k, h], to(1 - h, d))
        return carry

    lax.fori_loop(0, BLOCKS, relay, 0)

    def finish(k, carry):
        for h in (0, 1):
            arrived(ar2.at[k, h, 0:3], r_ar2.at[k, h], s_ar2.at[k, h])
            total = ar2[k, h, 0].astype(F32)
            for s in (1, 2, 3):
                total += ar2[k, h, s].astype(F32)
            image_t[32 * h:32 * h + 32, at(BLOCK * k, BLOCK, BLOCK)] = total
        return carry

    query, key = slice(0, RQ), slice(RQ, ROWS)

    def in_two(rows):
        image_h[0:64, rows] = image_t[:, rows].astype(BF16)
        image_h[64:128, rows] = (image_t[:, rows] - image_h[0:64, rows].astype(F32)).astype(BF16)

    def project(rows, start, width):
        p = dot(image_h[:, rows], merged[rows, at(start, width, 128)])
        return p[0:64] + p[64:128]

    def hand_over(side, rows):
        p = project(rows, (1 - c) * HALF, HALF)
        ranks = slice(64 * side, 64 * side + 64)
        for n in range(3):
            psend[n, ranks, :] = p[:, PART * n:PART * n + PART].astype(BF16)
            send(psend.at[n, ranks], psib.at[n, ranks], s_p.at[side, n], r_p.at[side, n], device(dc=1))

    lax.fori_loop(0, 2, finish, 0)
    in_two(query)
    hand_over(0, query)
    qown[...] = project(query, c * HALF, HALF)
    finish(2, 0)
    in_two(key)
    hand_over(1, key)

    def split(k):
        first, last = lax.div(2 - k, 2), lax.div(k, 2)
        return first, 1 - first - last, last

    def place(k):
        first, middle, last = split(k)
        return z * (1 - last) + y * last, y * first + x * (1 - first), x * first + y * middle + z * last

    def turned(v):
        return [lax.rem(v + d, 4) for d in range(4)]

    zs, ys, xs = turned(z), turned(y), turned(x)

    def plane(k):
        first, middle, last = split(k)
        far = range(4)
        dp_a = [(4 * zs[d] + y * middle) * (1 - last) + (4 * z + ys[d]) * last for d in far]
        dp_b = [ys[d] * first for d in far]
        tensor_b = [2 * (x * first + xs[d] * (1 - first)) + c for d in far]
        rows_a = [32 * (zs[d] * (1 - last) + ys[d] * last) for d in far]
        b = [ys[d] * first + xs[d] * (1 - first) for d in far]
        rows_b = [16 * lax.div(v, 2) for v in b]
        lanes_b = [LANES * lax.rem(v, 2) for v in b]

        def peer(da, db):
            return dp_a[da] + dp_b[db], tensor_b[db]

        def spot(da, db):
            return at(rows_a[da] + rows_b[db], 16, 16), lanes_b[db]

        return peer, spot

    def along(k, d):
        first, middle, last = split(k)
        return device(d * last, d * middle, d * first)

    around = [(da, db) for da in range(4) for db in range(4) if (da, db) != (0, 0)]
    around.sort(key=lambda o: -(min(o[0], 4 - o[0]) + min(o[1], 4 - o[1])))

    def share(k, carry):
        kk = project(key, c * HALF + PART * k, PART)
        for side in (0, 1):
            arrived(psib.at[k, 64 * side:64 * side + 64], r_p.at[side, k], s_p.at[side, k])
        pown[k, 0:64, :] = (qown[:, at(PART * k, PART, 128)] + psib[k, 0:64, :].astype(F32)).astype(BF16)
        pown[k, 64:128, :] = (kk + psib[k, 64:128, :].astype(F32)).astype(BF16)
        a, b, _ = place(k)
        peer, spot = plane(k)
        for da, db in around:
            rows, lanes = spot(da, db)
            send(pown.at[k, rows, at(lanes, LANES, 128)], rs.at[k, 4 * a + b], s_rs.at[k], r_rs.at[k], peer(da, db))
        rows, lanes = spot(0, 0)
        rs[k, 4 * a + b] = pown[k, rows, at(lanes, LANES, 128)]

        return carry

    lax.fori_loop(0, 3, share, 0)

    high = lax.Precision.HIGHEST
    tq, tk = image_t[:, 0:RQ], image_t[:, RQ:ROWS]
    gsend[...] = jnp.concatenate([dot(tq, tq, 1, 1, high), dot(tk, tk, 1, 1, high)], axis=1)
    send(gsend, gsib, s_g, r_g, device(dc=1))
    arrived(gsib, r_g, s_g)
    gx[x] = gsend[...] + gsib[...]
    for d in (2, 1, 3):
        send(gx.at[x], gx.at[x], s_gx, r_gx, device(dx=d))

    def gather(k, carry):
        arrived(rs.at[k, 0:15], r_rs.at[k], s_rs.at[k])
        total = rs[k, 0].astype(F32)
        for s in range(1, 16):
            total += rs[k, s].astype(F32)
        m = place(k)[2]
        ar3[k, m] = total.astype(BF16)
        for d in (2, 1, 3):
            send(ar3.at[k, m], ar3.at[k, m], s_a3.at[k], r_a3.at[k], along(k, d))
        return carry

    lax.fori_loop(0, 3, gather, 0)

    def spread(k, carry):
        arrived(ar3.at[k, 0:3], r_a3.at[k], s_a3.at[k])
        total = ar3[k, 0].astype(F32)
        for s in (1, 2, 3):
            total += ar3[k, s].astype(F32)
        peer, spot = plane(k)
        rows, lanes = spot(0, 0)
        here = (rows, at(c * HALF + PART * k + lanes, LANES, 128))
        psum[here] = total.astype(BF16)
        for da, db in around:
            send(psum.at[here], psum.at[here], s_ag.at[k], r_ag.at[k], peer(da, db))
        return carry

    lax.fori_loop(0, 3, spread, 0)

    arrived(gx.at[0:3], r_gx, s_gx)
    gsib[...] = (gx[0] + gx[1]) + (gx[2] + gx[3])
    factorize(gsib, inv)
    both = inv[...]
    for side, rows in ((0, slice(0, RQ)), (1, slice(RQ, ROWS))):
        w = both[:, 64 * side:64 * side + 64]
        basis[rows, :] = dot(image_t[:, rows], w, 0, 1, high).astype(BF16) * 0.0625
        hi = w.astype(BF16)
        white[side, 0:64] = hi
        white[side, 64:128] = (w - hi.astype(F32)).astype(BF16)

    def whiten(k, carry):
        arrived(rs.at[k, 0:15], r_ag.at[k], s_ag.at[k])
        cols = at(c * HALF + PART * k, PART, 128)
        for side in (0, 1):
            f = dot(white[side], psum[64 * side:64 * side + 64, cols])
            factor[64 * side:64 * side + 64, cols] = (f[0:64] + f[64:128]).astype(BF16)
        send(factor.at[:, cols], factor.at[:, cols], s_fw.at[k], r_fw.at[k], device(dc=1))
        return carry

    lax.fori_loop(0, 3, whiten, 0)

    def errors(k, carry):
        start = c * HALF + PART * k
        subtract(merged, merged, basis, factor, start, start)
        return carry

    lax.fori_loop(0, 3, errors, 0)

    sent(gsend, r_g, s_g)
    sent(gx.at[0:3], r_gx, s_gx)
    for k in range(BLOCKS):
        for h in (0, 1):
            sent(ar1.at[k, h, 0:3], r_ar1.at[k, h], s_ar1.at[k, h])
            sent(ar2.at[k, h, 0:3], r_ar2.at[k, h], s_ar2.at[k, h])
    for k in range(3):
        for side in (0, 1):
            sent(psend.at[k, 64 * side:64 * side + 64], r_p.at[side, k], s_p.at[side, k])
        sent(rs.at[k, 0:15], r_rs.at[k], s_rs.at[k])
        sent(ar3.at[k, 0:3], r_a3.at[k], s_a3.at[k])
        sent(rs.at[k, 0:15], r_ag.at[k], s_ag.at[k])
    for k in range(3):
        arrived(psend.at[k], r_fw.at[k], s_fw.at[k])
        sent(psend.at[k], r_fw.at[k], s_fw.at[k])


def reduce(gq, gk, eq, ek, fq, fk):
    dma, vmem = pltpu.SemaphoreType.DMA, pltpu.VMEM
    return pl.pallas_call(
        reduce_kernel,
        name="reduce",
        out_shape=(
            vmem((ROWS, D), BF16),
            vmem((ROWS, RANK), BF16),
            vmem((2 * RANK, D), BF16),
        ),
        in_specs=[pl.BlockSpec(memory_space=pltpu.HBM)] * 6,
        out_specs=(pl.BlockSpec(memory_space=vmem),) * 3,
        scratch_shapes=[
            vmem((2 * RANK, D), BF16),
            vmem((RANK, 128), F32),
            vmem((2, 128, RANK), BF16),
            vmem((ROWS, D), BF16),
            vmem((2, RANK, D), BF16),
            vmem((BLOCKS, 2, 4, 32, BLOCK), BF16),
            vmem((BLOCKS, 2, 4, 32, BLOCK), BF16),
            vmem((RANK, ROWS), F32),
            vmem((2 * RANK, ROWS), BF16),
            vmem((RANK, 128), F32),
            vmem((RANK, 128), F32),
            vmem((4, RANK, 128), F32),
            vmem((RANK, HALF), F32),
            vmem((3, 128, PART), BF16),
            vmem((3, 128, PART), BF16),
            vmem((3, 128, PART), BF16),
            vmem((3, 16, 16, LANES), BF16),
            vmem((3, 4, 16, LANES), BF16),
            dma((BLOCKS,)), dma,
            dma((BLOCKS, 2)), dma((BLOCKS, 2)), dma((BLOCKS, 2)), dma((BLOCKS, 2)),
            dma, dma, dma, dma,
            dma((2, 3)), dma((2, 3)), dma((3,)), dma((3,)), dma((3,)), dma((3,)),
            dma((3,)), dma((3,)), dma((3,)), dma((3,)),
        ],
        compiler_params=pltpu.CompilerParams(
            collective_id=0, has_side_effects=True, vmem_limit_bytes=53 << 20
        ),
    )(gq, gk, eq, ek, fq, fk)


def refresh_kernel(merged, basis, factor, error_q, error_k, new_q, new_k, buf, sem):
    c = lax.rem(lax.axis_index("tensor"), 2)
    own, other = c * HALF, (1 - c) * HALF
    mine = at(own, HALF, 128)
    copies = [
        pltpu.make_async_copy(merged.at[0:RQ, mine], error_q.at[0, 0, :, mine], sem.at[0]),
        pltpu.make_async_copy(merged.at[RQ:ROWS, mine], error_k.at[0, 0, :, mine], sem.at[1]),
        pltpu.make_async_copy(factor.at[0:RANK], new_q.at[0], sem.at[2]),
        pltpu.make_async_copy(factor.at[RANK:2 * RANK], new_k.at[0], sem.at[3]),
    ]
    for cp in copies:
        cp.start()
    def part(k):
        here, there = at(PART * k, PART, 128), at(other + PART * k, PART, 128)
        return [
            pltpu.make_async_copy(buf.at[0:RQ, here], error_q.at[0, 0, :, there], sem.at[4 + 2 * k]),
            pltpu.make_async_copy(buf.at[RQ:ROWS, here], error_k.at[0, 0, :, there], sem.at[5 + 2 * k]),
        ]

    def errors(k, carry):
        subtract(merged, buf, basis, factor, other + PART * k, PART * k)
        for cp in part(k):
            cp.start()
        return carry

    lax.fori_loop(0, 3, errors, 0)
    for k in range(3):
        copies += part(k)
    for cp in copies:
        cp.wait()


def refresh(merged, basis, factor):
    return pl.pallas_call(
        refresh_kernel,
        name="refresh",
        out_shape=(
            jax.ShapeDtypeStruct((1, 1, RQ, D), BF16),
            jax.ShapeDtypeStruct((1, 1, RK, D), BF16),
            jax.ShapeDtypeStruct((1, RANK, D), BF16),
            jax.ShapeDtypeStruct((1, RANK, D), BF16),
        ),
        in_specs=[pl.BlockSpec(memory_space=pltpu.VMEM)] * 3,
        out_specs=(pl.BlockSpec(memory_space=pltpu.HBM),) * 4,
        scratch_shapes=[pltpu.VMEM((ROWS, HALF), BF16), pltpu.SemaphoreType.DMA((10,))],
        compiler_params=pltpu.CompilerParams(vmem_limit_bytes=16 << 20),
    )(merged, basis, factor)


def body(grad_query, grad_key, error_query, error_key, factor_query, factor_key):
    fq, fk = jnp.swapaxes(factor_query, 1, 2), jnp.swapaxes(factor_key, 1, 2)
    kept = reduce(grad_query, grad_key, error_query, error_key, fq, fk)
    new_eq, new_ek, new_q, new_k = refresh(*kept)
    return new_eq, new_ek, jnp.swapaxes(new_q, 1, 2), jnp.swapaxes(new_k, 1, 2)


def solution(mesh):
    split = P("dp", None, "tensor", None)
    return jax.shard_map(
        body,
        mesh=mesh,
        in_specs=(split, split, split, split, P(), P()),
        out_specs=(split, split, P(), P()),
        check_vma=False,
    )
```

```python
import jax
import jax.numpy as jnp
from jax import lax
from jax.experimental import pallas as pl
from jax.experimental.pallas import tpu as pltpu
from jax.sharding import PartitionSpec as P

F32, BF16 = jnp.float32, jnp.bfloat16
D, RANK = 4608, 64
RQ, RK = 512, 256
ROWS = RQ + RK
BLOCK = 256
BLOCKS = ROWS // BLOCK
HALF = D // 2
PART = HALF // 3
LANES = PART // 2
MESH = pl.DeviceIdType.MESH


def dot(a, b, ca=1, cb=0, precision=None):
    return lax.dot_general(a, b, (((ca,), (cb,)), ((), ())), precision=precision, preferred_element_type=F32)


def at(start, size, unit):
    return pl.ds(pl.multiple_of(start, unit), size)


def factorize(gram, inv):
    lane = lax.broadcasted_iota(jnp.int32, (8, 128), 1)
    row = lax.broadcasted_iota(jnp.int32, (8, 128), 0)
    side = jnp.where(lane >= RANK, RANK, 0)
    for i in range(8):
        inv[8 * i:8 * i + 8, :] = jnp.where(lane - side == row + 8 * i, 1.0, 0.0).astype(F32)

    def column(x, j):
        return jnp.take_along_axis(x, side + j, axis=1, mode="promise_in_bounds")

    def block(b, carry):
        here = at(8 * b, 8, 8)
        g = [gram[here, :]] + [gram[8 * i:8 * i + 8, :] for i in range(8)]
        w = [inv[here, :]] + [inv[8 * i:8 * i + 8, :] for i in range(8)]
        done = [None] * 8
        for t in range(0, 8, 2):
            j = 8 * b + t
            row_g0, row_g1 = (jnp.broadcast_to(g[0][r:r + 1, :], (8, 128)) for r in (t, t + 1))
            row_w0, row_w1 = (jnp.broadcast_to(w[0][r:r + 1, :], (8, 128)) for r in (t, t + 1))
            pivot0, beside, pivot1 = column(row_g0, j), column(row_g0, j + 1), column(row_g1, j + 1)
            inverse0 = 1.0 / pivot0
            ratio = beside * inverse0
            pivot1 = pivot1 - ratio * beside
            inverse1 = 1.0 / pivot1
            row_g1, row_w1 = row_g1 - ratio * row_g0, row_w1 - ratio * row_w0
            done[t], done[t + 1] = row_w0 * lax.rsqrt(pivot0), row_w1 * lax.rsqrt(pivot1)
            scaled_g0, scaled_w0 = row_g0 * inverse0, row_w0 * inverse0
            scaled_g1, scaled_w1 = row_g1 * inverse1, row_w1 * inverse1
            for i in range(9):
                c0, c1 = column(g[i], j), column(g[i], j + 1)
                c1 = c1 - ratio * c0
                c0 = jnp.where(row > t if i == 0 else i - 1 > b, c0, 0.0)
                c1 = jnp.where(row > t + 1 if i == 0 else i - 1 > b, c1, 0.0)
                g[i] = g[i] - c0 * scaled_g0 - c1 * scaled_g1
                w[i] = w[i] - c0 * scaled_w0 - c1 * scaled_w1
        last = done[0]
        for t in range(1, 8):
            last = jnp.where(row == t, done[t], last)
        for i in range(8):
            gram[8 * i:8 * i + 8, :] = g[i + 1]
            inv[8 * i:8 * i + 8, :] = w[i + 1]
        inv[here, :] = last
        return carry

    lax.fori_loop(0, 8, block, 0)


def subtract(source, target, basis, factor, start, into):
    cols, there = at(start, PART, 128), at(into, PART, 128)
    for side, rows in ((0, slice(0, RQ)), (1, slice(RQ, ROWS))):
        approx = dot(basis[rows, :], factor[64 * side:64 * side + 64, cols])
        target[rows, there] = (source[rows, cols].astype(F32) - approx).astype(BF16)


def reduce_kernel(gq, gk, eq, ek, fq, fk, merged, basis, factor,
                  psum, inv, white, ebuf, fbuf, ar1, ar2, image_t, image_h,
                  gsend, gsib, gx, qown, psend, psib, pown, rs, ar3,
                  lsem, fsem, s_ar1, r_ar1, s_ar2, r_ar2, s_g, r_g, s_gx, r_gx,
                  s_p, r_p, s_rs, r_rs, s_a3, r_a3, s_ag, r_ag, s_fw, r_fw):
    dp, tensor = lax.axis_index("dp"), lax.axis_index("tensor")
    z, y = lax.div(dp, 4), lax.rem(dp, 4)
    x, c = lax.div(tensor, 2), lax.rem(tensor, 2)

    def device(dz=0, dy=0, dx=0, dc=0):
        return (lax.rem(z + dz, 4) * 4 + lax.rem(y + dy, 4), lax.rem(x + dx, 4) * 2 + lax.rem(c + dc, 2))

    def send(src, dst, ssem, rsem, to):
        pltpu.make_async_remote_copy(src, dst, ssem, rsem, device_id=to, device_id_type=MESH).start()

    def arrived(ref, rsem, ssem):
        pltpu.make_async_remote_copy(ref, ref, ssem, rsem, device_id=device(dc=1), device_id_type=MESH).wait_recv()

    def sent(ref, rsem, ssem):
        pltpu.make_async_remote_copy(ref, ref, ssem, rsem, device_id=device(dc=1), device_id_type=MESH).wait_send()

    loads = [
        pltpu.make_async_copy(fq.at[0], fbuf.at[0], fsem),
        pltpu.make_async_copy(fk.at[0], fbuf.at[1], fsem),
    ]
    for cp in loads:
        cp.start()

    for k, (grad, error, row) in enumerate(((gq, eq, 0), (gq, eq, BLOCK), (gk, ek, 0))):
        rows, there = pl.ds(row, BLOCK), pl.ds(BLOCK * k, BLOCK)
        pltpu.make_async_copy(grad.at[0, 0, rows], merged.at[there], lsem.at[k]).start()
        pltpu.make_async_copy(error.at[0, 0, rows], ebuf.at[there], lsem.at[k]).start()

    offsets = [(a, b, d) for a in range(4) for b in range(4) for d in range(4) if (a, b, d) != (0, 0, 0) and 0 in (a, b, d)]
    barrier = pltpu.get_barrier_semaphore()
    peers = [device(a, b, d) for a, b, d in offsets] + [device(dc=1)]
    for to in peers:
        pl.semaphore_signal(barrier, 1, device_id=to, device_id_type=MESH)

    first, second = (z, y), (y, z)

    def to(h, d):
        return device(dz=d) if h == 0 else device(dy=d)

    for cp in loads:
        cp.wait()

    def merge(k, carry):
        rows = at(BLOCK * k, BLOCK, BLOCK)
        pltpu.make_async_copy(gk.at[0, 0], merged.at[rows], lsem.at[k]).wait()
        pltpu.make_async_copy(ek.at[0, 0], ebuf.at[rows], lsem.at[k]).wait()
        merged[rows, :] = (merged[rows, :].astype(F32) + ebuf[rows, :].astype(F32)).astype(BF16)
        part = dot(fbuf[lax.div(k, 2)], merged[rows, :], 1, 1)

        @pl.when(k == 0)
        def _():
            pl.semaphore_wait(barrier, len(peers))

        for h in (0, 1):
            mine = ar1.at[k, h, first[h]]
            mine[...] = part[32 * h:32 * h + 32].astype(BF16)
            for d in (2, 1, 3):
                send(mine, mine, s_ar1.at[k, h], r_ar1.at[k, h], to(h, d))
        return carry

    lax.fori_loop(0, BLOCKS, merge, 0)

    def relay(k, carry):
        for h in (0, 1):
            arrived(ar1.at[k, h, 0:3], r_ar1.at[k, h], s_ar1.at[k, h])
            total = ar1[k, h, 0].astype(F32)
            for s in (1, 2, 3):
                total += ar1[k, h, s].astype(F32)
            mine = ar2.at[k, h, second[h]]
            mine[...] = total.astype(BF16)
            for d in (2, 1, 3):
                send(mine, mine, s_ar2.at[k, h], r_ar2.at[k, h], to(1 - h, d))
        return carry

    lax.fori_loop(0, BLOCKS, relay, 0)

    def finish(k, carry):
        for h in (0, 1):
            arrived(ar2.at[k, h, 0:3], r_ar2.at[k, h], s_ar2.at[k, h])
            total = ar2[k, h, 0].astype(F32)
            for s in (1, 2, 3):
                total += ar2[k, h, s].astype(F32)
            image_t[32 * h:32 * h + 32, at(BLOCK * k, BLOCK, BLOCK)] = total
        return carry

    query, key = slice(0, RQ), slice(RQ, ROWS)

    def in_two(rows):
        image_h[0:64, rows] = image_t[:, rows].astype(BF16)
        image_h[64:128, rows] = (image_t[:, rows] - image_h[0:64, rows].astype(F32)).astype(BF16)

    def project(rows, start, width):
        p = dot(image_h[:, rows], merged[rows, at(start, width, 128)])
        return p[0:64] + p[64:128]

    def hand_over(side, rows):
        p = project(rows, (1 - c) * HALF, HALF)
        ranks = slice(64 * side, 64 * side + 64)
        for n in range(3):
            psend[n, ranks, :] = p[:, PART * n:PART * n + PART].astype(BF16)
            send(psend.at[n, ranks], psib.at[n, ranks], s_p.at[side, n], r_p.at[side, n], device(dc=1))

    lax.fori_loop(0, 2, finish, 0)
    in_two(query)
    hand_over(0, query)
    qown[...] = project(query, c * HALF, HALF)
    finish(2, 0)
    in_two(key)
    hand_over(1, key)

    def split(k):
        first, last = lax.div(2 - k, 2), lax.div(k, 2)
        return first, 1 - first - last, last

    def place(k):
        first, middle, last = split(k)
        return z * (1 - last) + y * last, y * first + x * (1 - first), x * first + y * middle + z * last

    def turned(v):
        return [lax.rem(v + d * (1 - 2 * c) + 4, 4) for d in range(4)]

    zs, ys, xs = turned(z), turned(y), turned(x)

    def plane(k):
        first, middle, last = split(k)
        far = range(4)
        dp_a = [(4 * zs[d] + y * middle) * (1 - last) + (4 * z + ys[d]) * last for d in far]
        dp_b = [ys[d] * first for d in far]
        tensor_b = [2 * (x * first + xs[d] * (1 - first)) + c for d in far]
        rows_a = [32 * (zs[d] * (1 - last) + ys[d] * last) for d in far]
        b = [ys[d] * first + xs[d] * (1 - first) for d in far]
        rows_b = [16 * lax.div(v, 2) for v in b]
        lanes_b = [LANES * lax.rem(v, 2) for v in b]

        def peer(da, db):
            return dp_a[da] + dp_b[db], tensor_b[db]

        def spot(da, db):
            return at(rows_a[da] + rows_b[db], 16, 16), lanes_b[db]

        return peer, spot

    def along(k, d):
        first, middle, last = split(k)
        return device(d * last, d * middle, d * first)

    around = [(da, db) for da in range(4) for db in range(4) if (da, db) != (0, 0)]
    around.sort(key=lambda o: -(min(o[0], 4 - o[0]) + min(o[1], 4 - o[1])))

    def share(k, carry):
        kk = project(key, c * HALF + PART * k, PART)
        for side in (0, 1):
            arrived(psib.at[k, 64 * side:64 * side + 64], r_p.at[side, k], s_p.at[side, k])
        pown[k, 0:64, :] = (qown[:, at(PART * k, PART, 128)] + psib[k, 0:64, :].astype(F32)).astype(BF16)
        pown[k, 64:128, :] = (kk + psib[k, 64:128, :].astype(F32)).astype(BF16)
        a, b, _ = place(k)
        peer, spot = plane(k)
        for da, db in around:
            rows, lanes = spot(da, db)
            send(pown.at[k, rows, at(lanes, LANES, 128)], rs.at[k, 4 * a + b], s_rs.at[k], r_rs.at[k], peer(da, db))
        rows, lanes = spot(0, 0)
        rs[k, 4 * a + b] = pown[k, rows, at(lanes, LANES, 128)]

        return carry

    lax.fori_loop(0, 3, share, 0)

    high = lax.Precision.HIGHEST
    tq, tk = image_t[:, 0:RQ], image_t[:, RQ:ROWS]
    gsend[...] = jnp.concatenate([dot(tq, tq, 1, 1, high), dot(tk, tk, 1, 1, high)], axis=1)
    send(gsend, gsib, s_g, r_g, device(dc=1))
    arrived(gsib, r_g, s_g)
    gx[x] = gsend[...] + gsib[...]
    for d in (2, 1, 3):
        send(gx.at[x], gx.at[x], s_gx, r_gx, device(dx=d))

    def gather(k, carry):
        arrived(rs.at[k, 0:15], r_rs.at[k], s_rs.at[k])
        total = rs[k, 0].astype(F32)
        for s in range(1, 16):
            total += rs[k, s].astype(F32)
        m = place(k)[2]
        ar3[k, m] = total.astype(BF16)
        for d in (2, 1, 3):
            send(ar3.at[k, m], ar3.at[k, m], s_a3.at[k], r_a3.at[k], along(k, d))
        return carry

    lax.fori_loop(0, 3, gather, 0)

    def spread(k, carry):
        arrived(ar3.at[k, 0:3], r_a3.at[k], s_a3.at[k])
        total = ar3[k, 0].astype(F32)
        for s in (1, 2, 3):
            total += ar3[k, s].astype(F32)
        peer, spot = plane(k)
        rows, lanes = spot(0, 0)
        here = (rows, at(c * HALF + PART * k + lanes, LANES, 128))
        psum[here] = total.astype(BF16)
        for da, db in around:
            send(psum.at[here], psum.at[here], s_ag.at[k], r_ag.at[k], peer(da, db))
        return carry

    lax.fori_loop(0, 3, spread, 0)

    arrived(gx.at[0:3], r_gx, s_gx)
    gsib[...] = (gx[0] + gx[1]) + (gx[2] + gx[3])
    factorize(gsib, inv)
    both = inv[...]
    for side, rows in ((0, slice(0, RQ)), (1, slice(RQ, ROWS))):
        w = both[:, 64 * side:64 * side + 64]
        basis[rows, :] = dot(image_t[:, rows], w, 0, 1, high).astype(BF16) * 0.0625
        hi = w.astype(BF16)
        white[side, 0:64] = hi
        white[side, 64:128] = (w - hi.astype(F32)).astype(BF16)

    def whiten(k, carry):
        arrived(rs.at[k, 0:15], r_ag.at[k], s_ag.at[k])
        cols = at(c * HALF + PART * k, PART, 128)
        for side in (0, 1):
            f = dot(white[side], psum[64 * side:64 * side + 64, cols])
            factor[64 * side:64 * side + 64, cols] = (f[0:64] + f[64:128]).astype(BF16)
        send(factor.at[:, cols], factor.at[:, cols], s_fw.at[k], r_fw.at[k], device(dc=1))
        return carry

    lax.fori_loop(0, 3, whiten, 0)

    def errors(k, carry):
        start = c * HALF + PART * k
        subtract(merged, merged, basis, factor, start, start)
        return carry

    lax.fori_loop(0, 3, errors, 0)

    sent(gsend, r_g, s_g)
    sent(gx.at[0:3], r_gx, s_gx)
    for k in range(BLOCKS):
        for h in (0, 1):
            sent(ar1.at[k, h, 0:3], r_ar1.at[k, h], s_ar1.at[k, h])
            sent(ar2.at[k, h, 0:3], r_ar2.at[k, h], s_ar2.at[k, h])
    for k in range(3):
        for side in (0, 1):
            sent(psend.at[k, 64 * side:64 * side + 64], r_p.at[side, k], s_p.at[side, k])
        sent(rs.at[k, 0:15], r_rs.at[k], s_rs.at[k])
        sent(ar3.at[k, 0:3], r_a3.at[k], s_a3.at[k])
        sent(rs.at[k, 0:15], r_ag.at[k], s_ag.at[k])
    for k in range(3):
        arrived(psend.at[k], r_fw.at[k], s_fw.at[k])
        sent(psend.at[k], r_fw.at[k], s_fw.at[k])


def reduce(gq, gk, eq, ek, fq, fk):
    dma, vmem = pltpu.SemaphoreType.DMA, pltpu.VMEM
    return pl.pallas_call(
        reduce_kernel,
        name="reduce",
        out_shape=(
            vmem((ROWS, D), BF16),
            vmem((ROWS, RANK), BF16),
            vmem((2 * RANK, D), BF16),
        ),
        in_specs=[pl.BlockSpec(memory_space=pltpu.HBM)] * 6,
        out_specs=(pl.BlockSpec(memory_space=vmem),) * 3,
        scratch_shapes=[
            vmem((2 * RANK, D), BF16),
            vmem((RANK, 128), F32),
            vmem((2, 128, RANK), BF16),
            vmem((ROWS, D), BF16),
            vmem((2, RANK, D), BF16),
            vmem((BLOCKS, 2, 4, 32, BLOCK), BF16),
            vmem((BLOCKS, 2, 4, 32, BLOCK), BF16),
            vmem((RANK, ROWS), F32),
            vmem((2 * RANK, ROWS), BF16),
            vmem((RANK, 128), F32),
            vmem((RANK, 128), F32),
            vmem((4, RANK, 128), F32),
            vmem((RANK, HALF), F32),
            vmem((3, 128, PART), BF16),
            vmem((3, 128, PART), BF16),
            vmem((3, 128, PART), BF16),
            vmem((3, 16, 16, LANES), BF16),
            vmem((3, 4, 16, LANES), BF16),
            dma((BLOCKS,)), dma,
            dma((BLOCKS, 2)), dma((BLOCKS, 2)), dma((BLOCKS, 2)), dma((BLOCKS, 2)),
            dma, dma, dma, dma,
            dma((2, 3)), dma((2, 3)), dma((3,)), dma((3,)), dma((3,)), dma((3,)),
            dma((3,)), dma((3,)), dma((3,)), dma((3,)),
        ],
        compiler_params=pltpu.CompilerParams(
            collective_id=0, has_side_effects=True, vmem_limit_bytes=53 << 20
        ),
    )(gq, gk, eq, ek, fq, fk)


def refresh_kernel(merged, basis, factor, error_q, error_k, new_q, new_k, buf, sem):
    c = lax.rem(lax.axis_index("tensor"), 2)
    own, other = c * HALF, (1 - c) * HALF
    mine = at(own, HALF, 128)
    copies = [
        pltpu.make_async_copy(merged.at[0:RQ, mine], error_q.at[0, 0, :, mine], sem.at[0]),
        pltpu.make_async_copy(merged.at[RQ:ROWS, mine], error_k.at[0, 0, :, mine], sem.at[1]),
        pltpu.make_async_copy(factor.at[0:RANK], new_q.at[0], sem.at[2]),
        pltpu.make_async_copy(factor.at[RANK:2 * RANK], new_k.at[0], sem.at[3]),
    ]
    for cp in copies:
        cp.start()
    def part(k):
        here, there = at(PART * k, PART, 128), at(other + PART * k, PART, 128)
        return [
            pltpu.make_async_copy(buf.at[0:RQ, here], error_q.at[0, 0, :, there], sem.at[4 + 2 * k]),
            pltpu.make_async_copy(buf.at[RQ:ROWS, here], error_k.at[0, 0, :, there], sem.at[5 + 2 * k]),
        ]

    def errors(k, carry):
        subtract(merged, buf, basis, factor, other + PART * k, PART * k)
        for cp in part(k):
            cp.start()
        return carry

    lax.fori_loop(0, 3, errors, 0)
    for k in range(3):
        copies += part(k)
    for cp in copies:
        cp.wait()


def refresh(merged, basis, factor):
    return pl.pallas_call(
        refresh_kernel,
        name="refresh",
        out_shape=(
            jax.ShapeDtypeStruct((1, 1, RQ, D), BF16),
            jax.ShapeDtypeStruct((1, 1, RK, D), BF16),
            jax.ShapeDtypeStruct((1, RANK, D), BF16),
            jax.ShapeDtypeStruct((1, RANK, D), BF16),
        ),
        in_specs=[pl.BlockSpec(memory_space=pltpu.VMEM)] * 3,
        out_specs=(pl.BlockSpec(memory_space=pltpu.HBM),) * 4,
        scratch_shapes=[pltpu.VMEM((ROWS, HALF), BF16), pltpu.SemaphoreType.DMA((10,))],
        compiler_params=pltpu.CompilerParams(vmem_limit_bytes=16 << 20),
    )(merged, basis, factor)


def body(grad_query, grad_key, error_query, error_key, factor_query, factor_key):
    fq, fk = jnp.swapaxes(factor_query, 1, 2), jnp.swapaxes(factor_key, 1, 2)
    kept = reduce(grad_query, grad_key, error_query, error_key, fq, fk)
    new_eq, new_ek, new_q, new_k = refresh(*kept)
    return new_eq, new_ek, jnp.swapaxes(new_q, 1, 2), jnp.swapaxes(new_k, 1, 2)


def solution(mesh):
    split = P("dp", None, "tensor", None)
    return jax.shard_map(
        body,
        mesh=mesh,
        in_specs=(split, split, split, split, P(), P()),
        out_specs=(split, split, P(), P()),
        check_vma=False,
    )
```
